128 devices in a mesh: freq: 4 (over y), space: 32 (over x, z, core).
Axes of the slice: x: 4, y: 4, z: 4, core: 2. Of those that a mesh axis runs over, the one named last changes fastest.
Arguments:
- boundary_power_density: bfloat16 [32, 524288], P(None, ('freq', 'space')), may hold values from -6 to 6
- face_scales: bfloat16 [524288], P(('freq', 'space')), may hold values from 0.5 to 5
- face_node: int32 [524288], P(('freq', 'space')), may hold values from 0 to 511
- send_counts: int32 [4096], P(('freq', 'space')), may hold values from 1 to 128, as said below
- tile_values: bfloat16 [4096, 8, 128, 128], P('space')
- tile_mask: int32 [4096, 8], P('space'), may hold values from 0 to 1, as said below
- tile_columns: int32 [4096, 8], P('space'), may hold values from 0 to 135, as said below
- film_sink: float32 [524288], P('space'), may hold values from 0.01 to 0.2
- capacity: float32 [524288], P('space'), may hold values from 0.1 to 1
Outputs:
- surface_harmonics: float32 [32, 65536], P('freq', 'space')
- temperature: float32 [32, 524288], P('freq', 'space')
The draws below stay inside these ranges and needn't reach their ends.
Inputs may be any that keep to these rules, and one draw needn't show every extreme that they name: `send_counts`: every fluid device sends exactly 128 live slots to one partition, the same for all fluid devices in a draw. `tile_mask`: slot 0 of each row tile is live. `tile_columns`: row tile r of a partition (counted in it) names distinct extended tiles of r to r + 8, slot 0 naming r + 4.
All inputs are finite; a program needn't handle non-finite values.
Results may differ from the reference program's by a relative error of at most 0.0011.
Values may be sent and summed in bfloat16 or wider, within the bound.
No kernel may reach another device: no remote copies, remote signals or barrier semaphores. Data moves between devices by JAX's collectives and lax.ppermute only.
A program may use at most 128 MiB of HBM per device.

```python
import math
import jax
import jax.numpy as jnp
from jax import lax

LEVELS = 32
CAP = 128
BOUNDARY_PER_CPU = 512
NODES_DEV = 16384
TILE = 128
SLOTS = 8
HALO_TILES = 4
SWEEPS = 8
FACE_SLOTS = 524288
SURF_ALL = 65536
NODES = 524288
ROW_TILES = 4096
N_FREQ = 4
N_SPACE = 32


def draw_send_counts(key, part):
    key = jax.random.fold_in(key, 14)
    key_hot, key_rest = jax.random.split(key)
    total = N_FREQ * N_SPACE * N_SPACE
    hottest = jax.random.randint(key_hot, (), 0, N_SPACE)
    others = jax.random.randint(key_rest, (total,), 1, 3 * CAP // 4 + 1)
    position = jnp.arange(total, dtype=jnp.int32) % N_SPACE
    return jnp.where(position == hottest, CAP, others).astype(jnp.int32)


def draw_tile_columns(key, part):
    key = jax.random.fold_in(key, 11)
    per_part = NODES_DEV // TILE
    count = NODES // TILE
    local_row = jnp.arange(count, dtype=jnp.int32) % per_part
    breadth = 2 * HALO_TILES
    scores = jax.random.randint(key, (count, breadth), 0, 1 << 20) * breadth + jnp.arange(breadth, dtype=jnp.int32)[None, :]
    chosen = jnp.argsort(scores, axis=1)[:, :SLOTS - 1].astype(jnp.int32)
    offset = jnp.where(chosen < HALO_TILES, chosen - HALO_TILES, chosen - HALO_TILES + 1)
    centre_tile = local_row + HALO_TILES
    return jnp.concatenate([centre_tile[:, None], centre_tile[:, None] + offset], axis=1).astype(jnp.int32)


def draw_tile_mask(key, part):
    key = jax.random.fold_in(key, 12)
    count = NODES // TILE
    live = (jax.random.randint(key, (count, SLOTS), 0, 4) < 3).astype(jnp.int32)
    return live.at[:, 0].set(1)


def draw_tile_values(key, part):
    key = jax.random.fold_in(key, 13)
    count = NODES // TILE
    uniform_part = jax.random.uniform(key, (count, SLOTS, TILE, TILE), jnp.float32)
    coupling = 1.6 / (TILE * SLOTS)
    values = uniform_part * coupling
    return values.astype(jnp.bfloat16)


def with_ends(entries, own_key, smallest, largest):
    extent = entries.shape
    index_at = [jax.random.randint(jax.random.fold_in(own_key, axis), (), 0, extent[axis]) for axis in range(len(extent))]
    entries = entries.at[tuple(index_at)].set(smallest)
    longest = extent.index(max(extent))
    index_at[longest] = (index_at[longest] + 1) % extent[longest]
    return entries.at[tuple(index_at)].set(largest)


def shard_levels(own_key, dims, shards, low, high):
    level = 1.0
    for dim, blocks in shards:
        draws = jax.random.uniform(jax.random.fold_in(jax.random.fold_in(own_key, 6), dim), (blocks,), jnp.float32, low / len(shards), high / len(shards))
        level = level * jnp.repeat(jnp.exp(draws), dims[dim] // blocks).reshape((-1,) + (1,) * (len(dims) - 1 - dim))
    return level


def scatter_about(key, shape, scale, most, shards=(), held_as=jnp.bfloat16):
    drawn = jax.random.normal(key, shape, jnp.float32) * scale
    if len(shards) > 0:
        drawn = shard_levels(key, shape, shards, -0.22, 0.18) * drawn
    return jnp.clip(drawn, min=-most, max=most).astype(held_as)


def setup_inputs(seed: int = 0) -> dict:
    arg_keys = jax.random.split(jax.random.key(seed), 10)
    boundary_power_density = scatter_about(arg_keys[0], (LEVELS, FACE_SLOTS), 1.0, 6.0, ((1, 128),))
    face_scales = jnp.clip(jnp.exp(math.log(5.0) - 2.3025851 * jax.random.uniform(arg_keys[1], (FACE_SLOTS,), jnp.float32) ** shard_levels(arg_keys[1], (FACE_SLOTS,), ((0, 128),), -0.2, 0.2)), 0.5, 5.0).astype(jnp.bfloat16)
    face_node = with_ends(jax.random.randint(arg_keys[2], (FACE_SLOTS,), 0, BOUNDARY_PER_CPU), jax.random.fold_in(arg_keys[2], 1), 0, BOUNDARY_PER_CPU - 1).astype(jnp.int32)
    send_counts = draw_send_counts(jax.random.fold_in(arg_keys[9], 71), 0)
    tile_values = draw_tile_values(jax.random.fold_in(arg_keys[9], 71), 0)
    tile_mask = draw_tile_mask(jax.random.fold_in(arg_keys[9], 71), 0)
    tile_columns = draw_tile_columns(jax.random.fold_in(arg_keys[9], 71), 0)
    film_sink = jnp.clip(jnp.exp(math.log(0.2) - 2.9957323 * jax.random.uniform(arg_keys[7], (NODES,), jnp.float32) ** shard_levels(arg_keys[7], (NODES,), ((0, 32),), -0.2, 0.2)), 0.01, 0.2)
    capacity = jnp.clip(jnp.exp(math.log(1.0) - 2.3025851 * jax.random.uniform(arg_keys[8], (NODES,), jnp.float32) ** shard_levels(arg_keys[8], (NODES,), ((0, 32),), -0.2, 0.2)), 0.1, 1.0)
    return dict(boundary_power_density=boundary_power_density, face_scales=face_scales, face_node=face_node, send_counts=send_counts, tile_values=tile_values, tile_mask=tile_mask, tile_columns=tile_columns, film_sink=film_sink, capacity=capacity)


LOW_EDGE = 0.05
HIGH_EDGE = 2.0
FREQUENCY_SPACING = 0.003


def fourier_matrix(thermal_states):
    harmonic_part = jnp.arange(thermal_states, dtype=jnp.int32)
    position_couple = (harmonic_part // 2).astype(jnp.float32)
    parity = harmonic_part % 2
    instant_grid = jnp.arange(thermal_states, dtype=jnp.int32).astype(jnp.float32)
    cycle_argument = (2.0 * math.pi / thermal_states) * position_couple[:, None] * instant_grid[None, :]
    cosine_vector = jnp.where(position_couple[:, None] == 0, 1.0 / thermal_states, (2.0 / thermal_states) * jnp.cos(cycle_argument))
    odd_wave_weights = jnp.where(position_couple[:, None] == 0, jnp.cos(math.pi * instant_grid)[None, :] / thermal_states, (-2.0 / thermal_states) * jnp.sin(cycle_argument))
    return jnp.where(parity[:, None] == 1, odd_wave_weights, cosine_vector).astype(jnp.float32)


def rotate(vector_in):
    halves = vector_in.reshape(vector_in.shape[0] // 2, 2, vector_in.shape[1])
    return jnp.stack([-halves[:, 1], halves[:, 0]], axis=1).reshape(vector_in.shape)


def reference(boundary_power_density, face_scales, face_node, send_counts, tile_values, tile_mask, tile_columns, film_sink, capacity):
    opening_total = boundary_power_density.shape[1]
    slot_index = jnp.arange(opening_total, dtype=jnp.int32)
    source_block = slot_index // (N_SPACE * CAP)
    source_group = source_block // N_SPACE
    target_part = (slot_index // CAP) % N_SPACE
    send_limit = send_counts[source_block * N_SPACE + target_part]
    weight = jnp.where(slot_index % CAP < send_limit, face_scales, jnp.zeros_like(face_scales))
    target = target_part * (N_FREQ * BOUNDARY_PER_CPU) + source_group * BOUNDARY_PER_CPU + face_node
    weighted = boundary_power_density.astype(jnp.float32) * weight.astype(jnp.float32)[None, :]
    level_sums = jnp.zeros((LEVELS, SURF_ALL), jnp.float32).at[:, target].add(weighted)
    surface = jnp.dot(fourier_matrix(LEVELS), level_sums, precision=lax.Precision.HIGHEST)
    surf_part = N_FREQ * BOUNDARY_PER_CPU
    rhs = jnp.pad(surface.reshape(LEVELS, N_SPACE, surf_part), ((0, 0), (0, 0), (0, NODES_DEV - surf_part))).reshape(LEVELS, NODES)

    row_tiles = NODES_DEV // TILE
    part_ids = jnp.arange(N_SPACE, dtype=jnp.int32)

    def part_rowsum(part_index):
        tiles_here = lax.dynamic_slice_in_dim(tile_values, part_index * row_tiles, row_tiles, 0).astype(jnp.float32)
        mask_here = lax.dynamic_slice_in_dim(tile_mask, part_index * row_tiles, row_tiles, 0).astype(jnp.float32)
        return jnp.einsum('rtij,rt->ri', tiles_here, mask_here, precision=lax.Precision.HIGHEST)

    rowsum = lax.map(part_rowsum, part_ids).reshape(NODES)
    diagonal = rowsum + film_sink
    strength = FREQUENCY_SPACING * (jnp.arange(LEVELS, dtype=jnp.int32) // 2).astype(jnp.float32)

    def coupling(rounded):
        padded = jnp.pad(rounded, ((0, 0), (HALO_TILES * TILE, HALO_TILES * TILE)))
        blocks = padded.reshape(LEVELS, ROW_TILES + 2 * HALO_TILES, TILE)

        def one_part(part_index):
            extended = lax.dynamic_slice_in_dim(blocks, part_index * row_tiles, row_tiles + 2 * HALO_TILES, 1)
            columns = lax.dynamic_slice_in_dim(tile_columns, part_index * row_tiles, row_tiles, 0)
            mask_here = lax.dynamic_slice_in_dim(tile_mask, part_index * row_tiles, row_tiles, 0).astype(jnp.float32)
            tiles_here = lax.dynamic_slice_in_dim(tile_values, part_index * row_tiles, row_tiles, 0).astype(jnp.float32)
            picked = extended[:, columns].astype(jnp.float32) * mask_here[None, :, :, None]
            return jnp.einsum('crtj,rtij->cri', picked, tiles_here, precision=lax.Precision.HIGHEST)

        result = lax.map(one_part, part_ids)
        return jnp.transpose(result, (1, 0, 2, 3)).reshape(LEVELS, NODES)

    def apply(vector_in):
        coupled = coupling(vector_in.astype(jnp.bfloat16))
        return diagonal[None, :] * vector_in - coupled + strength[:, None] * capacity[None, :] * rotate(vector_in)

    centre = 0.5 * (HIGH_EDGE + LOW_EDGE)
    half_width = 0.5 * (HIGH_EDGE - LOW_EDGE)
    stretch = centre / half_width
    previous = 1.0 / stretch
    solution = jnp.zeros((LEVELS, NODES), jnp.float32)
    residual = rhs
    direction = residual / (centre * diagonal[None, :])
    for sweep in range(SWEEPS):
        solution = solution + direction
        if sweep + 1 < SWEEPS:
            residual = residual - apply(direction)
            current = 1.0 / (2.0 * stretch - previous)
            direction = (current * previous) * direction + (2.0 * current / half_width) * residual / diagonal[None, :]
            previous = current
    return surface, solution
```

```python
import math

import jax
import jax.numpy as jnp
import numpy as np
from jax import lax
from jax.experimental import pallas as pl
from jax.experimental.pallas import tpu as pltpu
from jax.sharding import PartitionSpec as P

SUB = 512
TILE = 128
SLOTS = 8
HALO = 4
SWEEPS = 8
COMPS = 8
LEVELS = 32

LOW_EDGE = 0.05
HIGH_EDGE = 2.0
FREQUENCY_SPACING = 0.003

STEPS = SWEEPS - 1
SURF_TILES = 16
HEAD = SURF_TILES + HALO * STEPS
TAIL = HALO * STEPS
LEND = 12
PACK = 48

F32 = jnp.float32
BF16 = jnp.bfloat16


def fourier_table():
    row = np.arange(LEVELS)
    p = (row // 2).astype(np.float64)[:, None]
    n = np.arange(LEVELS, dtype=np.float64)[None, :]
    angle = 2.0 * math.pi / LEVELS * p * n
    even = np.where(p == 0, 1.0 / LEVELS, 2.0 / LEVELS * np.cos(angle))
    odd = np.where(p == 0, np.cos(math.pi * n) / LEVELS, -2.0 / LEVELS * np.sin(angle))
    return np.where((row % 2 == 1)[:, None], odd, even).astype(np.float32)


def chebyshev_scalars():
    centre = 0.5 * (HIGH_EDGE + LOW_EDGE)
    half = 0.5 * (HIGH_EDGE - LOW_EDGE)
    stretch = centre / half
    previous = 1.0 / stretch
    scalars = []
    for _ in range(STEPS):
        current = 1.0 / (2.0 * stretch - previous)
        scalars.append((current * previous, 2.0 * current / half))
        previous = current
    return centre, scalars


def pack_kernel(counts, power, scales, nodes, out):
    targets = out.shape[0]
    row = lax.broadcasted_iota(jnp.int32, (16, TILE), 0)
    lane = lax.broadcasted_iota(jnp.int32, (16, TILE), 1)
    for d in range(targets):
        out[d, :LEVELS, :] = power[:, d * TILE : (d + 1) * TILE]
        scale = jnp.broadcast_to(scales[d : d + 1, :], (16, TILE))
        node = jnp.broadcast_to(nodes[d : d + 1, :], (16, TILE))
        weight = jnp.where(lane < counts[d], scale, 0.0)
        high = (node >> 5).astype(F32)
        low = (node & 31).astype(F32)
        aux = jnp.where(row == 0, weight, jnp.where(row == 1, high, low))
        out[d, LEVELS:, :] = aux.astype(BF16)


def scatter_kernel(table, got, out):
    sources = got.shape[0]
    place = lax.broadcasted_iota(jnp.int32, (SUB, TILE), 0).astype(F32)

    def spread(s):
        aux = got[s, LEVELS:, :].astype(F32)
        node = aux[1:2, :] * 32.0 + aux[2:3, :]
        weight = jnp.broadcast_to(aux[0:1, :], (SUB, TILE))
        hit = jnp.broadcast_to(node, (SUB, TILE)) == place
        return jnp.where(hit, weight, 0.0).astype(BF16)

    def body(i, total):
        a, b = 2 * i, 2 * i + 1
        left = jnp.concatenate([got[a, :LEVELS, :], got[b, :LEVELS, :]], axis=1)
        right = jnp.concatenate([spread(a), spread(b)], axis=1)
        return total + lax.dot_general(
            left, right, (((1,), (1,)), ((), ())), preferred_element_type=F32
        )

    sums = lax.fori_loop(0, sources // 2, body, jnp.zeros((LEVELS, SUB), F32))
    surface = jnp.dot(
        table[...], sums, precision=lax.Precision.HIGHEST, preferred_element_type=F32
    )
    for f in range(out.shape[0]):
        out[f] = surface[f * COMPS : (f + 1) * COMPS, :]


def rotated(v):
    even = lax.broadcasted_iota(jnp.int32, v.shape, 0) % 2 == 0
    return jnp.where(even, -pltpu.roll(v, COMPS - 1, 0), pltpu.roll(v, 1, 0))


def strengths(group):
    comp = lax.broadcasted_iota(jnp.int32, (COMPS, TILE), 0) + group * COMPS
    return FREQUENCY_SPACING * (comp // 2).astype(F32)


def row_product(table, tiles, vector, i):
    total = None
    for t in range(0, SLOTS, 2):
        left = jnp.concatenate([vector[table[i, t]], vector[table[i, t + 1]]], axis=1)
        right = jnp.concatenate([tiles[i, t], tiles[i, t + 1]], axis=1)
        part = lax.dot_general(
            left, right, (((1,), (1,)), ((), ())), preferred_element_type=F32
        )
        total = part if total is None else total + part
    return total


def with_ones(v):
    return jnp.concatenate([v, jnp.ones((COMPS, TILE), F32)], axis=0).astype(BF16)


def clear(vectors, count):
    blank = with_ones(jnp.zeros((COMPS, TILE), F32))

    def body(i, carry):
        vectors[0, i] = blank
        vectors[1, i] = blank
        return carry

    lax.fori_loop(0, count, body, 0)
    nothing = jnp.zeros((2 * COMPS, TILE), BF16)
    vectors[0, count] = nothing
    vectors[1, count] = nothing


def sweep_rows(first, last, table, tiles, vectors, old, film, heat, strength, direction,
               residual, total, offset, scalars):
    keep, gain = scalars

    def one(i):
        product = row_product(table, tiles, vectors.at[old], i)
        diag = product[COMPS:, :] + film[pl.ds(i, 1), :]
        v = direction[i]
        mv = diag * v - product[:COMPS, :] + strength * heat[pl.ds(i, 1), :] * rotated(v)
        r = residual[i] - mv
        new = keep * v + gain * r / diag
        return r, new

    def body(q, carry):
        base = q * HALO
        results = [one(base + j) for j in range(HALO)]
        for j, (r, new) in enumerate(results):
            i = base + j
            residual[i] = r
            direction[i] = new
            vectors[1 - old, i + offset] = with_ones(new)
            total[i] = total[i] + new
        return carry

    lax.fori_loop(first // HALO, last // HALO, body, 0)


def head_kernel(table, group, surface, film, heat, tiles_hbm, lent_hbm, surface_out, head_out,
                edge_out, tiles, vectors, direction, residual, total, edges, sems):
    chunks = (LEND + HEAD) // HALO
    lent_chunks = LEND // HALO

    def copy(q):
        rows = pl.ds(q * HALO, HALO)
        if q < lent_chunks:
            source = lent_hbm.at[rows]
        else:
            source = tiles_hbm.at[pl.ds((q - lent_chunks) * HALO, HALO)]
        return pltpu.make_async_copy(source, tiles.at[rows], sems.at[q])

    surf_chunks = SURF_TILES // HALO
    order = [lent_chunks + q for q in range(surf_chunks)]
    for k in range(1, STEPS + 1):
        order.append(lent_chunks + surf_chunks + k - 1)
        if k <= lent_chunks:
            order.append(lent_chunks - k)
    assert sorted(order) == list(range(chunks))
    for q in order:
        copy(q).start()

    centre, scalars = chebyshev_scalars()
    strength = strengths(group[0])
    clear(vectors, LEND + HEAD + 2 * HALO)
    zero = jnp.zeros((COMPS, TILE), F32)

    def blank(i, carry):
        direction[i] = zero
        residual[i] = zero
        total[i] = zero
        return carry

    lax.fori_loop(0, LEND + HEAD, blank, 0)

    for j in range(SURF_TILES):
        part = surface[j // HALO, :, (j % HALO) * TILE : (j % HALO + 1) * TILE]
        surface_out[:, j * TILE : (j + 1) * TILE] = part
        residual[LEND + j] = part

    for q in range(surf_chunks):
        copy(lent_chunks + q).wait()

    def start(q, carry):
        base = LEND + q * HALO
        products = [row_product(table, tiles, vectors.at[1], base + j) for j in range(HALO)]
        for j, product in enumerate(products):
            i = base + j
            diag = product[COMPS:, :] + film[pl.ds(i, 1), :]
            new = residual[i] / (centre * diag)
            direction[i] = new
            total[i] = new
            vectors[0, i + HALO] = with_ones(new)
        return carry

    lax.fori_loop(0, surf_chunks, start, 0)
    for j in range(HALO):
        edges[0, j] = direction[LEND + j]

    for k in range(1, STEPS + 1):
        copy(lent_chunks + surf_chunks + k - 1).wait()
        if k <= lent_chunks:
            copy(lent_chunks - k).wait()
        low = LEND - HALO * min(k, STEPS - k)
        high = LEND + SURF_TILES + HALO * k
        sweep_rows(low, high, table, tiles, vectors, (k - 1) % 2, film, heat, strength, direction,
                   residual, total, HALO, scalars[k - 1])
        for j in range(HALO):
            edges[k, j] = direction[LEND + j]

    for j in range(HEAD):
        head_out[:, j * TILE : (j + 1) * TILE] = total[LEND + j]
    for p in range(SWEEPS // 2):
        for j in range(HALO):
            edge_out[p, j] = jnp.concatenate([edges[2 * p, j], edges[2 * p + 1, j]], axis=0).astype(BF16)


def tail_kernel(table, group, edge, film, heat, head, tiles_hbm, out, tiles, vectors, direction,
                residual, total, sems):
    row_tiles = out.shape[1] // TILE
    first = row_tiles - TAIL
    chunks = TAIL // HALO

    def copy(q):
        rows = pl.ds(q * HALO, HALO)
        source = tiles_hbm.at[pl.ds(first + q * HALO, HALO)]
        return pltpu.make_async_copy(source, tiles.at[rows], sems.at[q])

    for q in reversed(range(chunks)):
        copy(q).start()

    _, scalars = chebyshev_scalars()
    strength = strengths(group[0])
    clear(vectors, TAIL + 2 * HALO)
    zero = jnp.zeros((COMPS, TILE), F32)

    def blank(i, carry):
        direction[i] = zero
        residual[i] = zero
        total[i] = zero
        return carry

    lax.fori_loop(0, TAIL, blank, 0)
    out[:, : HEAD * TILE] = head[...]
    out[:, HEAD * TILE : first * TILE] = jnp.zeros((COMPS, (first - HEAD) * TILE), F32)

    for k in range(1, STEPS + 1):
        old = (k - 1) % 2
        for j in range(HALO):
            pair = edge[(k - 1) // 2, j].astype(F32)
            vectors[old, HALO + TAIL + j] = with_ones(pair[old * COMPS : (old + 1) * COMPS, :])
        copy(chunks - k).wait()
        sweep_rows(TAIL - HALO * k, TAIL, table, tiles, vectors, old, film, heat, strength,
                   direction, residual, total, HALO, scalars[k - 1])

    for j in range(TAIL):
        out[:, (first + j) * TILE : (first + j + 1) * TILE] = total[j]


def vmem():
    return pl.BlockSpec(memory_space=pltpu.VMEM)


def smem():
    return pl.BlockSpec(memory_space=pltpu.SMEM)


def hbm():
    return pl.BlockSpec(memory_space=pl.ANY)


def local(
    boundary_power_density,
    face_scales,
    face_node,
    send_counts,
    tile_values,
    tile_mask,
    tile_columns,
    film_sink,
    capacity,
):
    parts = lax.axis_size("space")
    groups = lax.axis_size("freq")
    place = lax.axis_index("space")
    group = lax.axis_index("freq").astype(jnp.int32).reshape(1)
    nodes_here = film_sink.shape[0]
    row_tiles = nodes_here // TILE
    up = [(i, i + 1) for i in range(parts - 1)]
    down = [(i + 1, i) for i in range(parts - 1)]

    film = film_sink.reshape(row_tiles, TILE)
    heat = capacity.reshape(row_tiles, TILE)

    lent = lax.ppermute(lax.slice_in_dim(tile_values, row_tiles - LEND, row_tiles), "space", up)
    places = jnp.where(tile_mask > 0, tile_columns, -1).astype(F32)
    facts = jnp.concatenate(
        [
            film[row_tiles - LEND :],
            heat[row_tiles - LEND :],
            jnp.pad(places[row_tiles - LEND :], ((0, 0), (0, TILE - SLOTS))),
        ],
        axis=0,
    )
    facts = lax.ppermute(facts, "space", up)
    lent_film = jnp.where(place == 0, 1.0, facts[:LEND])
    lent_places = facts[2 * LEND :, :SLOTS].astype(jnp.int32)
    blank = LEND + HEAD + 2 * HALO
    own = jnp.where(tile_mask > 0, tile_columns, -1)
    lent_table = jnp.where(
        (lent_places < 0) | (place == 0), blank, lent_places - (row_tiles - LEND)
    )
    head_own = own[:HEAD]
    head_table = jnp.concatenate(
        [lent_table, jnp.where(head_own < 0, blank, head_own + LEND)], axis=0
    )
    tail_own = own[row_tiles - TAIL :]
    tail_table = jnp.where(tail_own < 0, TAIL + 2 * HALO, tail_own - (row_tiles - TAIL))
    head_film = jnp.concatenate([lent_film, film[:HEAD]], axis=0)
    head_heat = jnp.concatenate([facts[LEND : 2 * LEND], heat[:HEAD]], axis=0)

    packed = pl.pallas_call(
        pack_kernel,
        out_shape=jax.ShapeDtypeStruct((parts, PACK, TILE), BF16),
        in_specs=[smem(), vmem(), vmem(), vmem()],
        out_specs=vmem(),
    )(
        send_counts,
        boundary_power_density,
        face_scales.reshape(parts, TILE).astype(F32),
        face_node.reshape(parts, TILE),
    )
    got = lax.all_to_all(packed, "space", 0, 0)
    mixed = pl.pallas_call(
        scatter_kernel,
        out_shape=jax.ShapeDtypeStruct((groups, COMPS, SUB), F32),
        in_specs=[vmem(), vmem()],
        out_specs=vmem(),
    )(jnp.asarray(fourier_table()), got)
    mixed = lax.all_to_all(mixed, "freq", 0, 0)

    rows = LEND + HEAD
    surface, head, edge = pl.pallas_call(
        head_kernel,
        out_shape=(
            jax.ShapeDtypeStruct((COMPS, SURF_TILES * TILE), F32),
            jax.ShapeDtypeStruct((COMPS, HEAD * TILE), F32),
            jax.ShapeDtypeStruct((SWEEPS // 2, HALO, 2 * COMPS, TILE), BF16),
        ),
        in_specs=[smem(), smem(), vmem(), vmem(), vmem(), hbm(), hbm()],
        out_specs=(vmem(), vmem(), vmem()),
        scratch_shapes=[
            pltpu.VMEM((rows, SLOTS, TILE, TILE), BF16),
            pltpu.VMEM((2, rows + 2 * HALO + 1, 2 * COMPS, TILE), BF16),
            pltpu.VMEM((rows, COMPS, TILE), F32),
            pltpu.VMEM((rows, COMPS, TILE), F32),
            pltpu.VMEM((rows, COMPS, TILE), F32),
            pltpu.VMEM((SWEEPS, HALO, COMPS, TILE), F32),
            pltpu.SemaphoreType.DMA((rows // HALO,)),
        ],
        compiler_params=pltpu.CompilerParams(vmem_limit_bytes=40 << 20),
    )(head_table, group, mixed, head_film, head_heat, tile_values, lent)

    edge = lax.ppermute(edge, "space", down)

    temperature = pl.pallas_call(
        tail_kernel,
        out_shape=jax.ShapeDtypeStruct((COMPS, nodes_here), F32),
        in_specs=[smem(), smem(), vmem(), vmem(), vmem(), vmem(), hbm()],
        out_specs=vmem(),
        scratch_shapes=[
            pltpu.VMEM((TAIL, SLOTS, TILE, TILE), BF16),
            pltpu.VMEM((2, TAIL + 2 * HALO + 1, 2 * COMPS, TILE), BF16),
            pltpu.VMEM((TAIL, COMPS, TILE), F32),
            pltpu.VMEM((TAIL, COMPS, TILE), F32),
            pltpu.VMEM((TAIL, COMPS, TILE), F32),
            pltpu.SemaphoreType.DMA((TAIL // HALO,)),
        ],
        compiler_params=pltpu.CompilerParams(vmem_limit_bytes=40 << 20),
    )(
        tail_table,
        group,
        edge,
        film[row_tiles - TAIL :],
        heat[row_tiles - TAIL :],
        head,
        tile_values,
    )
    return surface, temperature


def solution(mesh):
    placed = (
        P(None, ("freq", "space")),
        P(("freq", "space")),
        P(("freq", "space")),
        P(("freq", "space")),
        P("space", None, None, None),
        P("space", None),
        P("space", None),
        P("space"),
        P("space"),
    )
    return jax.shard_map(
        local,
        mesh=mesh,
        in_specs=placed,
        out_specs=(P("freq", "space"), P("freq", "space")),
        check_vma=False,
    )
```

```python
import math

import jax
import jax.numpy as jnp
import numpy as np
from jax import lax
from jax.experimental import pallas as pl
from jax.experimental.pallas import tpu as pltpu
from jax.sharding import PartitionSpec as P

SUB = 512
TILE = 128
SLOTS = 8
HALO = 4
SWEEPS = 8
COMPS = 8
LEVELS = 32

LOW_EDGE = 0.05
HIGH_EDGE = 2.0
FREQUENCY_SPACING = 0.003

STEPS = SWEEPS - 1
SURF_TILES = 16
HEAD = SURF_TILES + HALO * STEPS
TAIL = HALO * STEPS
LEND = 12
PIECES = (12,)
PACK = 48

HEAD_ROWS = LEND + HEAD
HEAD_BLANK = HEAD_ROWS + 2 * HALO
TAIL_BLANK = TAIL + 2 * HALO

F32 = jnp.float32
BF16 = jnp.bfloat16


def fourier_table():
    row = np.arange(LEVELS)
    p = (row // 2).astype(np.float64)[:, None]
    n = np.arange(LEVELS, dtype=np.float64)[None, :]
    angle = 2.0 * math.pi / LEVELS * p * n
    even = np.where(p == 0, 1.0 / LEVELS, 2.0 / LEVELS * np.cos(angle))
    odd = np.where(p == 0, np.cos(math.pi * n) / LEVELS, -2.0 / LEVELS * np.sin(angle))
    return np.where((row % 2 == 1)[:, None], odd, even).astype(np.float32)


CENTRE = 0.5 * (HIGH_EDGE + LOW_EDGE)


def chebyshev_scalars():
    half = 0.5 * (HIGH_EDGE - LOW_EDGE)
    stretch = CENTRE / half
    previous = 1.0 / stretch
    scalars = []
    for _ in range(STEPS):
        current = 1.0 / (2.0 * stretch - previous)
        scalars.append((current * previous, 2.0 * current / half))
        previous = current
    return scalars


def needs(task, low, high):
    k, g = task
    if k == 1:
        return []
    return [(k - 1, h) for h in (g - 1, g, g + 1) if low(k - 1) <= h <= high(k - 1)]


def in_order(tasks):
    steps = sorted({k for k, _ in tasks})
    return [sorted(t for t in tasks if t[0] == k) for k in steps]


def head_plan():
    def low(k):
        return -min(k, STEPS - k)

    def high(k):
        return 3 + k

    def reads(task):
        return needs(task, lambda k: -k, high)

    every = {(k, g) for k in range(1, STEPS + 1) for g in range(low(k), high(k) + 1)}
    free = set()
    for task in sorted(every):
        if task[1] >= 0 and all(n in free for n in reads(task)):
            free.add(task)
    return in_order(free), in_order(every - free)


def tail_plan():
    return [[(k, g) for g in range(-k, 0)] for k in range(1, STEPS + 1)]


def pack_kernel(counts, power, scales, nodes, columns, mask, film, heat, out, head_table, tail_table, facts):
    targets = out.shape[0]
    row_tiles = film.shape[0]
    row = lax.broadcasted_iota(jnp.int32, (16, TILE), 0)
    lane = lax.broadcasted_iota(jnp.int32, (16, TILE), 1)
    for d in range(targets):
        out[d, :LEVELS, :] = power[:, d * TILE : (d + 1) * TILE]
        scale = jnp.broadcast_to(scales[d : d + 1, :].astype(F32), (16, TILE))
        node = jnp.broadcast_to(nodes[d : d + 1, :], (16, TILE))
        weight = jnp.where(lane < counts[d], scale, 0.0)
        high = (node >> 5).astype(F32)
        low = (node & 31).astype(F32)
        aux = jnp.where(row == 0, weight, jnp.where(row == 1, high, low))
        out[d, LEVELS:, :] = aux.astype(BF16)
    live = mask[...] > 0
    head_table[...] = jnp.where(live, columns[...] + LEND, HEAD_BLANK)
    tail_table[...] = jnp.where(live, columns[...] - (row_tiles - TAIL), TAIL_BLANK)
    lent_table = jnp.where(live, columns[...] - (row_tiles - LEND), HEAD_BLANK)
    facts[:SLOTS, :] = lent_table.astype(F32)
    facts[SLOTS : SLOTS + LEND, :] = film[row_tiles - LEND :, :]
    facts[SLOTS + LEND :, :] = heat[row_tiles - LEND :, :]


def scatter_kernel(group, table, got, *rest):
    out, (sums, surface) = rest[:-2], rest[-2:]
    sources = got.shape[0]
    span = 8
    place = lax.broadcasted_iota(jnp.int32, (SUB, TILE), 0).astype(F32)

    def spread(s):
        aux = got[s, LEVELS:, :].astype(F32)
        node = aux[1:2, :] * 32.0 + aux[2:3, :]
        weight = jnp.broadcast_to(aux[0:1, :], (SUB, TILE))
        hit = jnp.broadcast_to(node, (SUB, TILE)) == place
        return jnp.where(hit, weight, 0.0).astype(BF16)

    sums[...] = jnp.zeros((LEVELS, SUB), F32)

    def body(i, carry):
        first = i * span
        left = jnp.concatenate([got[first + n, :LEVELS, :] for n in range(span)], axis=1)
        right = jnp.concatenate([spread(first + n) for n in range(span)], axis=1)
        sums[...] += lax.dot_general(
            left, right, (((1,), (1,)), ((), ())), preferred_element_type=F32
        )
        return carry

    lax.fori_loop(0, sources // span, body, 0)
    surface[...] = jnp.dot(
        table[...], sums[...], precision=lax.Precision.HIGHEST, preferred_element_type=F32
    )
    for shift in range(len(out)):
        f = lax.rem(group[0] + shift, len(out))
        out[shift][...] = surface[pl.ds(pl.multiple_of(f * COMPS, COMPS), COMPS), :]


def with_ones(v):
    return jnp.concatenate([v, jnp.ones((COMPS, TILE), F32)], axis=0).astype(BF16)


def lend_kernel(tiles_hbm, *rest):
    pieces, sems = rest[:-1], rest[-1]
    first = tiles_hbm.shape[0] - sum(piece.shape[0] for piece in pieces)
    copies = []
    for n, piece in enumerate(pieces):
        rows = pl.ds(first, piece.shape[0])
        copies.append(pltpu.make_async_copy(tiles_hbm.at[rows], piece, sems.at[n]))
        copies[-1].start()
        first += piece.shape[0]
    for copy in copies:
        copy.wait()


def transpose_tiles(first, tiles_hbm, out_hbm, buffer, tiles, sems, out_sem):
    depth = buffer.shape[0]
    chunks = tiles.shape[0] // HALO

    def copy(q, slot):
        return pltpu.make_async_copy(
            tiles_hbm.at[pl.ds(first + q * HALO, HALO)], buffer.at[slot], sems.at[slot]
        )

    def back(q):
        rows = pl.ds(q * HALO, HALO)
        return pltpu.make_async_copy(tiles.at[rows], out_hbm.at[rows], out_sem.at[q])

    for q in range(depth):
        copy(q, q).start()

    def chunk(q, carry):
        slot = lax.rem(q, depth)
        copy(q, slot).wait()
        for j in range(HALO):
            for t in range(SLOTS):
                tiles[q * HALO + j, t] = buffer[slot, j, t].T
        back(q).start()

        @pl.when(q + depth < chunks)
        def _():
            copy(q + depth, slot).start()

        return carry

    lax.fori_loop(0, chunks, chunk, 0)
    return [back(q) for q in range(chunks)]


def prep_kernel(mask, film, tiles_hbm, out_hbm, diag, buffer, tiles, sems, out_sem):
    copies = transpose_tiles(0, tiles_hbm, out_hbm, buffer, tiles, sems, out_sem)

    def sums(i, carry):
        rowsum = jnp.zeros((COMPS, TILE), F32)
        for t in range(SLOTS):
            tile = tiles[i, t].astype(F32).reshape(TILE // COMPS, COMPS, TILE)
            rowsum += jnp.sum(tile, axis=0) * mask[t, i].astype(F32)
        diag[i] = jnp.broadcast_to(
            jnp.sum(rowsum, axis=0, keepdims=True) + film[pl.ds(i, 1), :], (COMPS, TILE)
        )
        return carry

    lax.fori_loop(0, SURF_TILES, sums, 0)
    for copy in copies:
        copy.wait()


def rotated(v):
    even = lax.broadcasted_iota(jnp.int32, v.shape, 0) % 2 == 0
    return jnp.where(even, -pltpu.roll(v, COMPS - 1, 0), pltpu.roll(v, 1, 0))


def strengths(group):
    comp = lax.broadcasted_iota(jnp.int32, (COMPS, TILE), 0) + group * COMPS
    return FREQUENCY_SPACING * (comp // 2).astype(F32)


class Rows:
    def __init__(self, groups, first, transposed, source, buffer, sems, table, film, heat, fact_row, table_row,
                 extra=0.0):
        self.transposed, self.table, self.film, self.heat = transposed, table, film, heat
        self.first, self.fact_row, self.table_row, self.extra = first, fact_row, table_row, extra
        self.buffer, self.slot, self.copies = buffer, {}, {}
        for n, g in enumerate(groups):
            rows = pl.ds(n * HALO, HALO)
            self.slot[g] = n * HALO
            self.copies[g] = pltpu.make_async_copy(source(g), buffer.at[rows], sems.at[first + n])

    def fetch(self, g):
        self.copies[g].start()

    def wait(self, g):
        copy = self.copies.pop(g, None)
        if copy is not None:
            copy.wait()

    def product(self, vector, g, j):
        i = self.slot[g] + j
        row = HALO * g + j + self.table_row
        left = jnp.concatenate([vector[self.table[t, row]] for t in range(SLOTS)], axis=1)
        right = jnp.concatenate(
            [self.buffer[i, t] for t in range(SLOTS)], axis=0 if self.transposed else 1
        )
        return lax.dot_general(
            left,
            right,
            (((1,), (0 if self.transposed else 1,)), ((), ())),
            preferred_element_type=F32,
        )

    def diagonal(self, product, g, j):
        row = HALO * g + j + self.fact_row
        return product[COMPS:, :] + (self.film[row : row + 1, :] + self.extra)

    def shift(self, strength, g, j):
        row = HALO * g + j + self.fact_row
        return strength * self.heat[row : row + 1, :]


def rows_from(ref, row):
    return lambda g: ref.at[pl.ds(HALO * g + row, HALO)]


def fetch_all(plan, where):
    seen = set()
    for tasks in plan:
        for _, g in tasks:
            if g not in seen:
                seen.add(g)
                where(g).fetch(g)


def advance(plan, where, shift, strength, vectors, direction, residual, total):
    scalars = chebyshev_scalars()
    for tasks in plan:
        k = tasks[0][0]
        keep, gain = scalars[k - 1]
        products = []
        for _, g in tasks:
            where(g).wait(g)
            products += [where(g).product(vectors[k - 1], g, j) for j in range(HALO)]
        for n, (_, g) in enumerate(tasks):
            for j in range(HALO):
                product, state = products[n * HALO + j], HALO * g + j + shift
                diag = where(g).diagonal(product, g, j)
                v = direction[state]
                mv = diag * v - product[:COMPS, :] + where(g).shift(strength, g, j) * rotated(v)
                r = residual[state] - mv
                new = keep * v + gain * r / diag
                total[state] = total[state] + new
                if k < STEPS:
                    residual[state] = r
                    direction[state] = new
                    vectors[k][HALO + state] = with_ones(new)


def split(refs, rows):
    vectors, fields = refs
    places = rows + 2 * HALO + 1
    return (
        [vectors.at[pl.ds(k * places, places)] for k in range(STEPS)],
        *[fields.at[pl.ds(n * rows, rows)] for n in range(3)],
    )


def state_shape(rows):
    return [
        ((STEPS * (rows + 2 * HALO + 1), 2 * COMPS, TILE), BF16),
        ((3 * rows, COMPS, TILE), F32),
    ]


def clear(fields, vectors, blank_place, blank_places):
    zero = jnp.zeros((COMPS, TILE), F32)

    def body(i, carry):
        fields[i] = zero
        return carry

    lax.fori_loop(0, fields.shape[0], body, 0)
    for k, vector in enumerate(vectors):
        vector[blank_place] = jnp.zeros((2 * COMPS, TILE), BF16)
        for place in blank_places(k):
            vector[place] = with_ones(zero)


FAST = 6


def first_kernel(plan, table, group, own, near, far, opposite, diag, film, heat, fast_hbm, tiles_hbm,
                 surface, vectors, fields, fast_buffer, slow_buffer, sems):
    vector, direction, residual, total = split((vectors, fields), HEAD_ROWS)
    groups = range(HEAD // HALO)
    fast = Rows(groups[:FAST], 0, True, rows_from(fast_hbm, 0), fast_buffer, sems, table, film, heat, 0, 0)
    slow = Rows(groups[FAST:], FAST, False, rows_from(tiles_hbm, 0), slow_buffer, sems, table, film, heat, 0, 0)

    def where(g):
        return fast if g < FAST else slow

    fetch_all(plan, where)

    def blank_places(k):
        above = HALO + LEND + SURF_TILES + HALO * k
        below = HALO + LEND - HALO * (k + 2)
        places = [0] + [above + j for j in range(2 * HALO)]
        return places + [below + j for j in range(2 * HALO) if 0 <= below + j < HALO + LEND]

    clear(fields, vector, HEAD_BLANK, blank_places)
    for shift, part in enumerate((own, near, far, opposite)):
        g = lax.rem(group[0] + 4 - shift, 4)
        surface[:, pl.ds(pl.multiple_of(g * SUB, SUB), SUB)] = part[...]
        for j in range(HALO):
            value = part[:, j * TILE : (j + 1) * TILE]
            i = g * HALO + j
            new = value / (CENTRE * diag[i])
            residual[LEND + i] = value
            direction[LEND + i] = new
            total[LEND + i] = new
            vector[0][HALO + LEND + i] = with_ones(new)
    advance(plan, where, LEND, strengths(group[0]), vector, direction, residual, total)


def second_kernel(plan, table, lent_table, place, group, film, heat, facts, vectors_in, fields_in, fast_hbm,
                  *rest):
    lent_hbm, rest = rest[: len(PIECES)], rest[len(PIECES) :]
    head, edge, vectors, fields, fast_buffer, lent_buffer, sems = rest
    vector, direction, residual, total = split((vectors, fields), HEAD_ROWS)
    first = (place[0] == 0).astype(F32)
    lent_groups = range(-LEND // HALO, 0)

    def lent_rows(g):
        row = HALO * g + LEND
        for piece, count in zip(lent_hbm, PIECES):
            if row < count:
                return piece.at[pl.ds(row, HALO)]
            row -= count

    lent = Rows(lent_groups, FAST, False, lent_rows, lent_buffer, sems, lent_table,
                facts.at[pl.ds(SLOTS, LEND)], facts.at[pl.ds(SLOTS + LEND, LEND)], LEND,
                table.shape[1], first)
    fast = Rows(range(FAST), 0, True, rows_from(fast_hbm, 0), fast_buffer, sems, table, film, heat, 0, 0)

    def where(g):
        return lent if g < 0 else fast

    fetch_all(plan, where)
    vectors[...] = vectors_in[...]
    fields[...] = fields_in[...]
    advance(plan, where, LEND, strengths(group[0]), vector, direction, residual, total)
    for k in range(0, STEPS, 2):
        for j in range(HALO):
            i = HALO + LEND + j
            a = vector[k][i].astype(F32)[:COMPS]
            b = vector[k + 1][i].astype(F32)[:COMPS] if k + 1 < STEPS else a
            edge[k // 2, j] = jnp.concatenate([a, b], axis=0).astype(BF16)
    for j in range(HEAD):
        head[:, j * TILE : (j + 1) * TILE] = total[LEND + j]


def tail_kernel(plan, table, group, edge, film, heat, head, tiles_hbm, out, vectors, fields, buffer, sems):
    vector, direction, residual, total = split((vectors, fields), TAIL)
    row_tiles = out.shape[1] // TILE
    first = row_tiles - TAIL
    rows = Rows(range(-TAIL // HALO, 0), 0, False, rows_from(tiles_hbm, row_tiles), buffer, sems, table, film, heat,
                row_tiles, row_tiles)

    def where(g):
        return rows

    fetch_all(plan, where)

    def blank_places(k):
        below = HALO + TAIL - HALO * (k + 2)
        return [below + j for j in range(2 * HALO)]

    clear(fields, vector, TAIL_BLANK, blank_places)
    for k in range(STEPS):
        for j in range(HALO):
            pair = edge[k // 2, j].astype(F32)
            half = pair[(k % 2) * COMPS : (k % 2 + 1) * COMPS, :]
            vector[k][HALO + TAIL + j] = with_ones(half)
    out[:, : HEAD * TILE] = head[...]
    out[:, HEAD * TILE : first * TILE] = jnp.zeros((COMPS, (first - HEAD) * TILE), F32)
    advance(plan, where, TAIL, strengths(group[0]), vector, direction, residual, total)
    for j in range(TAIL):
        out[:, (first + j) * TILE : (first + j + 1) * TILE] = total[j]


def vmem():
    return pl.BlockSpec(memory_space=pltpu.VMEM)


def smem():
    return pl.BlockSpec(memory_space=pltpu.SMEM)


def hbm():
    return pl.BlockSpec(memory_space=pltpu.HBM)


def in_hbm(*arrays):
    return [pltpu.with_memory_space_constraint(a, pltpu.HBM) for a in arrays]


def work(gigaflops):
    return pl.CostEstimate(flops=gigaflops * 10**9, bytes_accessed=0, transcendentals=0)


def kernel_params(mib):
    return pltpu.CompilerParams(vmem_limit_bytes=mib << 20)


def local(
    boundary_power_density,
    face_scales,
    face_node,
    send_counts,
    tile_values,
    tile_mask,
    tile_columns,
    film_sink,
    capacity,
):
    parts = lax.axis_size("space")
    groups = lax.axis_size("freq")
    place = lax.axis_index("space")
    group = lax.axis_index("freq").astype(jnp.int32).reshape(1)
    nodes_here = film_sink.shape[0]
    row_tiles = nodes_here // TILE
    up = [(i, i + 1) for i in range(parts - 1)]
    down = [(i + 1, i) for i in range(parts - 1)]
    first_plan, second_plan = head_plan()
    assert groups == 4

    tile_values = pltpu.with_memory_space_constraint(tile_values, pltpu.HBM)
    film = film_sink.reshape(row_tiles, TILE)
    heat = capacity.reshape(row_tiles, TILE)
    columns, mask = tile_columns.T, tile_mask.T

    def array(shape, dtype=F32):
        return jax.ShapeDtypeStruct(shape, dtype)

    packed, head_table, tail_table, facts = pl.pallas_call(
        pack_kernel,
        out_shape=(
            array((parts, PACK, TILE), BF16),
            array((SLOTS, row_tiles), jnp.int32),
            array((SLOTS, row_tiles), jnp.int32),
            array((SLOTS + 2 * LEND, TILE)),
        ),
        in_specs=[smem()] + [vmem()] * 7,
        out_specs=(vmem(),) * 4,
        compiler_params=kernel_params(8),
        name="pack",
    )(
        send_counts,
        *in_hbm(
            boundary_power_density,
            face_scales.reshape(parts, TILE),
            face_node.reshape(parts, TILE),
            columns,
            mask,
            film,
            heat,
        ),
    )
    got = lax.all_to_all(packed, "space", 0, 0)

    facts = lax.ppermute(facts, "space", up)
    lent = pl.pallas_call(
        lend_kernel,
        out_shape=[array((count, SLOTS, TILE, TILE), BF16) for count in PIECES],
        in_specs=[hbm()],
        out_specs=[vmem()] * len(PIECES),
        scratch_shapes=[pltpu.SemaphoreType.DMA((len(PIECES),))],
        compiler_params=kernel_params(8),
        cost_estimate=pl.CostEstimate(flops=0, bytes_accessed=6 << 20, transcendentals=0),
        name="lend",
    )(tile_values)
    lent = [lax.ppermute(piece, "space", up) for piece in lent]
    lent_table = facts[:SLOTS].astype(jnp.int32)

    depth = 4
    fast_tiles, diag = pl.pallas_call(
        prep_kernel,
        out_shape=(
            pltpu.HBM((FAST * HALO, SLOTS, TILE, TILE), BF16),
            array((SURF_TILES, COMPS, TILE)),
        ),
        in_specs=[smem(), vmem(), hbm()],
        out_specs=(hbm(), vmem()),
        scratch_shapes=[
            pltpu.VMEM((depth, HALO, SLOTS, TILE, TILE), BF16),
            pltpu.VMEM((FAST * HALO, SLOTS, TILE, TILE), BF16),
            pltpu.SemaphoreType.DMA((depth,)),
            pltpu.SemaphoreType.DMA((FAST,)),
        ],
        compiler_params=kernel_params(16),
        cost_estimate=pl.CostEstimate(flops=0, bytes_accessed=12 << 20, transcendentals=0),
        name="prep",
    )(mask, film, tile_values)

    (fast_tiles,) = in_hbm(fast_tiles)
    parts_of = pl.pallas_call(
        scatter_kernel,
        out_shape=(array((COMPS, SUB)),) * groups,
        in_specs=[smem(), vmem(), vmem()],
        out_specs=(vmem(),) * groups,
        scratch_shapes=[pltpu.VMEM((LEVELS, SUB), F32)] * 2,
        compiler_params=kernel_params(8),
        name="scatter",
    )(group, jnp.asarray(fourier_table()), got)
    mixed = [parts_of[0]] + [
        lax.ppermute(parts_of[s], "freq", [(i, (i + s) % groups) for i in range(groups)])
        for s in range(1, groups)
    ]

    held = state_shape(HEAD_ROWS)
    groups_here = HEAD // HALO

    def tile_buffer(count):
        return pltpu.VMEM((count * HALO, SLOTS, TILE, TILE), BF16)

    surface, *state = pl.pallas_call(
        lambda *refs: first_kernel(first_plan, *refs),
        out_shape=(array((COMPS, SURF_TILES * TILE)), *[array(*h) for h in held]),
        in_specs=[smem()] * 2 + [vmem()] * 7 + [hbm()] * 2,
        out_specs=(vmem(),) * 3,
        scratch_shapes=[
            tile_buffer(FAST),
            tile_buffer(groups_here - FAST),
            pltpu.SemaphoreType.DMA((groups_here,)),
        ],
        compiler_params=kernel_params(24),
        cost_estimate=work(200),
        name="first",
    )(head_table, group, *mixed, diag, film, heat, fast_tiles, tile_values)

    head, edge = pl.pallas_call(
        lambda *refs: second_kernel(second_plan, *refs),
        out_shape=(
            array((COMPS, HEAD * TILE)),
            array(((STEPS + 1) // 2, HALO, 2 * COMPS, TILE), BF16),
        ),
        in_specs=[smem()] * 4 + [vmem()] * 5 + [hbm()] * (1 + len(PIECES)),
        out_specs=(vmem(),) * 2,
        scratch_shapes=[
            *[pltpu.VMEM(*h) for h in held],
            tile_buffer(FAST),
            tile_buffer(LEND // HALO),
            pltpu.SemaphoreType.DMA((FAST + LEND // HALO,)),
        ],
        compiler_params=kernel_params(24),
        name="second",
    )(
        head_table,
        lent_table,
        place.astype(jnp.int32).reshape(1),
        group,
        film,
        heat,
        facts,
        *state,
        fast_tiles,
        *lent,
    )
    edge = lax.ppermute(edge, "space", down)

    temperature = pl.pallas_call(
        lambda *refs: tail_kernel(tail_plan(), *refs),
        out_shape=array((COMPS, nodes_here)),
        in_specs=[smem()] * 2 + [vmem()] * 4 + [hbm()],
        out_specs=vmem(),
        scratch_shapes=[
            *[pltpu.VMEM(*h) for h in state_shape(TAIL)],
            tile_buffer(TAIL // HALO),
            pltpu.SemaphoreType.DMA((TAIL // HALO,)),
        ],
        compiler_params=kernel_params(24),
        name="tail",
    )(tail_table, group, edge, film, heat, head, tile_values)
    return surface, temperature


def solution(mesh):
    placed = (
        P(None, ("freq", "space")),
        P(("freq", "space")),
        P(("freq", "space")),
        P(("freq", "space")),
        P("space", None, None, None),
        P("space", None),
        P("space", None),
        P("space"),
        P("space"),
    )
    return jax.shard_map(
        local,
        mesh=mesh,
        in_specs=placed,
        out_specs=(P("freq", "space"), P("freq", "space")),
        check_vma=False,
    )
```

```python
import math

import jax
import jax.numpy as jnp
import numpy as np
from jax import lax
from jax.experimental import pallas as pl
from jax.experimental.pallas import tpu as pltpu
from jax.sharding import PartitionSpec as P

SUB = 512
TILE = 128
SLOTS = 8
HALO = 4
SWEEPS = 8
COMPS = 8
LEVELS = 32

LOW_EDGE = 0.05
HIGH_EDGE = 2.0
FREQUENCY_SPACING = 0.003

STEPS = SWEEPS - 1
SURF_TILES = 16
HEAD = SURF_TILES + HALO * STEPS
TAIL = HALO * STEPS
LEND = 12
AHEAD = 4
PACK = 48

HEAD_ROWS = LEND + HEAD
HEAD_BLANK = HEAD_ROWS + 2 * HALO
TAIL_BLANK = TAIL + 2 * HALO

F32 = jnp.float32
BF16 = jnp.bfloat16


def fourier_table():
    row = np.arange(LEVELS)
    p = (row // 2).astype(np.float64)[:, None]
    n = np.arange(LEVELS, dtype=np.float64)[None, :]
    angle = 2.0 * math.pi / LEVELS * p * n
    even = np.where(p == 0, 1.0 / LEVELS, 2.0 / LEVELS * np.cos(angle))
    odd = np.where(p == 0, np.cos(math.pi * n) / LEVELS, -2.0 / LEVELS * np.sin(angle))
    return np.where((row % 2 == 1)[:, None], odd, even).astype(np.float32)


CENTRE = 0.5 * (HIGH_EDGE + LOW_EDGE)


def chebyshev_scalars():
    half = 0.5 * (HIGH_EDGE - LOW_EDGE)
    stretch = CENTRE / half
    previous = 1.0 / stretch
    scalars = []
    for _ in range(STEPS):
        current = 1.0 / (2.0 * stretch - previous)
        scalars.append((current * previous, 2.0 * current / half))
        previous = current
    return scalars


def needs(task, low, high):
    k, g = task
    if k == 1:
        return []
    return [(k - 1, h) for h in (g - 1, g, g + 1) if low(k - 1) <= h <= high(k - 1)]


def in_order(tasks):
    steps = sorted({k for k, _ in tasks})
    return [sorted(t for t in tasks if t[0] == k) for k in steps]


def head_plan():
    def low(k):
        return -min(k, STEPS - k)

    def high(k):
        return 3 + k

    def reads(task):
        return needs(task, lambda k: -k, high)

    every = {(k, g) for k in range(1, STEPS + 1) for g in range(low(k), high(k) + 1)}
    free = set()
    for task in sorted(every):
        if task[1] >= 0 and all(n in free for n in reads(task)):
            free.add(task)
    return in_order(free), in_order(every - free)


def tail_plan():
    return [[(k, g) for g in range(-k, 0)] for k in range(1, STEPS + 1)]


def copy_rows(tiles_hbm, first, out, sems):
    copies = []
    for n in range(out.shape[0]):
        copies.append(pltpu.make_async_copy(tiles_hbm.at[first + n], out.at[n], sems.at[n]))
        copies[-1].start()
    return copies


def lend_kernel(tiles_hbm, near, sems):
    for copy in copy_rows(tiles_hbm, tiles_hbm.shape[0] - LEND + AHEAD, near, sems):
        copy.wait()


def pack_kernel(counts, power, scales, nodes, mask, columns, film, heat, tiles_hbm, out, head_table, tail_table,
                facts, far, sems):
    row_tiles = film.shape[0]
    targets = out.shape[0]
    copies = copy_rows(tiles_hbm, row_tiles - LEND, far, sems)
    row = lax.broadcasted_iota(jnp.int32, (16, TILE), 0)
    lane = lax.broadcasted_iota(jnp.int32, (16, TILE), 1)
    for d in range(targets):
        out[d, :LEVELS, :] = power[:, d * TILE : (d + 1) * TILE]
        scale = jnp.broadcast_to(scales[d : d + 1, :].astype(F32), (16, TILE))
        node = jnp.broadcast_to(nodes[d : d + 1, :], (16, TILE))
        weight = jnp.where(lane < counts[d], scale, 0.0)
        high = (node >> 5).astype(F32)
        low = (node & 31).astype(F32)
        aux = jnp.where(row == 0, weight, jnp.where(row == 1, high, low))
        out[d, LEVELS:, :] = aux.astype(BF16)
    live = mask[...] > 0
    head_table[...] = jnp.where(live, columns[...] + LEND, HEAD_BLANK)
    tail_table[...] = jnp.where(live, columns[...] - (row_tiles - TAIL), TAIL_BLANK)
    lent_table = jnp.where(live, columns[...] - (row_tiles - LEND), HEAD_BLANK)
    facts[:SLOTS, :] = lent_table.astype(F32)
    facts[SLOTS : SLOTS + LEND, :] = film[row_tiles - LEND :, :]
    facts[SLOTS + LEND :, :] = heat[row_tiles - LEND :, :]
    for copy in copies:
        copy.wait()


def scatter_kernel(group, table, got, *rest):
    out, (sums, surface) = rest[:-2], rest[-2:]
    sources = got.shape[0]
    span = 8
    place = lax.broadcasted_iota(jnp.int32, (SUB, TILE), 0).astype(F32)

    def spread(s):
        aux = got[s, LEVELS:, :].astype(F32)
        node = aux[1:2, :] * 32.0 + aux[2:3, :]
        weight = jnp.broadcast_to(aux[0:1, :], (SUB, TILE))
        hit = jnp.broadcast_to(node, (SUB, TILE)) == place
        return jnp.where(hit, weight, 0.0).astype(BF16)

    sums[...] = jnp.zeros((LEVELS, SUB), F32)

    def body(i, carry):
        first = i * span
        left = jnp.concatenate([got[first + n, :LEVELS, :] for n in range(span)], axis=1)
        right = jnp.concatenate([spread(first + n) for n in range(span)], axis=1)
        sums[...] += lax.dot_general(
            left, right, (((1,), (1,)), ((), ())), preferred_element_type=F32
        )
        return carry

    lax.fori_loop(0, sources // span, body, 0)
    surface[...] = jnp.dot(
        table[...], sums[...], precision=lax.Precision.HIGHEST, preferred_element_type=F32
    )
    for shift in range(len(out)):
        f = lax.rem(group[0] + shift, len(out))
        out[shift][...] = surface[pl.ds(pl.multiple_of(f * COMPS, COMPS), COMPS), :]


def with_ones(v):
    return jnp.concatenate([v, jnp.ones((COMPS, TILE), F32)], axis=0).astype(BF16)


def rotated(v):
    even = lax.broadcasted_iota(jnp.int32, v.shape, 0) % 2 == 0
    return jnp.where(even, -pltpu.roll(v, COMPS - 1, 0), pltpu.roll(v, 1, 0))


def strengths(group):
    comp = lax.broadcasted_iota(jnp.int32, (COMPS, TILE), 0) + group * COMPS
    return FREQUENCY_SPACING * (comp // 2).astype(F32)


class Rows:
    def __init__(self, groups, table, film, heat, fact_row, table_row, extra=0.0, source=None, buffer=None,
                 sems=None, turned=None, turned_groups=(), ready=()):
        self.table, self.film, self.heat = table, film, heat
        self.fact_row, self.table_row, self.extra = fact_row, table_row, extra
        self.buffer, self.turned, self.ready = buffer, turned, set(ready)
        self.turned_slot = {g: n * HALO for n, g in enumerate(turned_groups)}
        self.slot, self.copies = {}, {}
        if source is not None:
            for n, g in enumerate(groups):
                self.slot[g] = n * HALO
                self.copies[g] = pltpu.make_async_copy(
                    source(g), buffer.at[pl.ds(n * HALO, HALO)], sems.at[n]
                )

    def fetch(self, g):
        if g in self.copies:
            self.copies[g].start()

    def wait(self, g):
        copy = self.copies.pop(g, None)
        if copy is not None:
            copy.wait()

    def turn(self, g, j):
        for t in range(SLOTS):
            self.turned[self.turned_slot[g] + j, t] = self.buffer[self.slot[g] + j, t].T

    def product(self, vector, g, j):
        row = HALO * g + j + self.table_row
        left = jnp.concatenate([vector[self.table[t, row]] for t in range(SLOTS)], axis=1)
        if g in self.ready:
            i = self.turned_slot[g] + j
            right = jnp.concatenate([self.turned[i, t] for t in range(SLOTS)], axis=0)
        else:
            i = self.slot[g] + j
            right = jnp.concatenate([self.buffer[i, t] for t in range(SLOTS)], axis=1)
        side = 0 if g in self.ready else 1
        return lax.dot_general(
            left, right, (((1,), (side,)), ((), ())), preferred_element_type=F32
        )

    def diagonal(self, product, g, j):
        row = HALO * g + j + self.fact_row
        return product[COMPS:, :] + (self.film[row : row + 1, :] + self.extra)

    def shift(self, strength, g, j):
        row = HALO * g + j + self.fact_row
        return strength * self.heat[row : row + 1, :]


def rows_from(ref, row):
    return lambda g: ref.at[pl.ds(HALO * g + row, HALO)]


def fetch_all(plan, where):
    seen = set()
    for tasks in plan:
        for _, g in tasks:
            if g not in seen:
                seen.add(g)
                where(g).fetch(g)


def advance(plan, where, shift, strength, vectors, direction, residual, total, keep_turned=(), rate=2):
    scalars = chebyshev_scalars()
    for n_step, tasks in enumerate(plan):
        k = tasks[0][0]
        keep, gain = scalars[k - 1]
        later = [g for step in plan[n_step + 1 :] for _, g in step] + list(keep_turned)
        fetched = {g for step in plan[: n_step + 1] for _, g in step}
        wanted = [
            g for g in fetched if g in later and g in where(g).turned_slot and g not in where(g).ready
        ]
        wanted = sorted(wanted, key=lambda g: -later.count(g))[:rate]
        turns = [(g, j) for g in wanted for j in range(HALO)]
        products = []
        for n, (_, g) in enumerate(tasks):
            where(g).wait(g)
            products += [where(g).product(vectors[k - 1], g, j) for j in range(HALO)]
            share = -(-len(turns) // len(tasks))
            for h, j in [t for t in turns[n * share : (n + 1) * share]]:
                where(h).wait(h)
                where(h).turn(h, j)
        for g in wanted:
            where(g).ready.add(g)
        for n, (_, g) in enumerate(tasks):
            for j in range(HALO):
                product, state = products[n * HALO + j], HALO * g + j + shift
                diag = where(g).diagonal(product, g, j)
                v = direction[state]
                mv = diag * v - product[:COMPS, :] + where(g).shift(strength, g, j) * rotated(v)
                r = residual[state] - mv
                new = keep * v + gain * r / diag
                total[state] = total[state] + new
                if k < STEPS:
                    residual[state] = r
                    direction[state] = new
                    vectors[k][HALO + state] = with_ones(new)
    for g in keep_turned:
        if g not in where(g).ready:
            for j in range(HALO):
                where(g).turn(g, j)


def split(refs, rows):
    vectors, fields = refs
    places = rows + 2 * HALO + 1
    return (
        [vectors.at[pl.ds(k * places, places)] for k in range(STEPS)],
        *[fields.at[pl.ds(n * rows, rows)] for n in range(3)],
    )


def state_shape(rows):
    return [
        ((STEPS * (rows + 2 * HALO + 1), 2 * COMPS, TILE), BF16),
        ((3 * rows, COMPS, TILE), F32),
    ]


def clear(fields, vectors, blank_place, blank_places):
    zero = jnp.zeros((COMPS, TILE), F32)

    def body(i, carry):
        fields[i] = zero
        return carry

    lax.fori_loop(0, fields.shape[0], body, 0)
    for k, vector in enumerate(vectors):
        vector[blank_place] = jnp.zeros((2 * COMPS, TILE), BF16)
        for place in blank_places(k):
            vector[place] = with_ones(zero)


FAST = 6
TURNED = 9


def first_kernel(plan, table, group, own, near, far, opposite, film, heat, tiles_hbm, after, surface, vectors, fields,
                 turned, buffer, sems):
    del after
    vector, direction, residual, total = split((vectors, fields), HEAD_ROWS)
    groups = range(HEAD // HALO)
    rows = Rows(groups, table, film, heat, 0, 0, source=rows_from(tiles_hbm, 0), buffer=buffer, sems=sems,
                turned=turned, turned_groups=groups[:TURNED])

    def where(g):
        return rows

    fetch_all(plan, where)

    def blank_places(k):
        above = HALO + LEND + SURF_TILES + HALO * k
        below = HALO + LEND - HALO * (k + 2)
        places = [0] + [above + j for j in range(2 * HALO)]
        return places + [below + j for j in range(2 * HALO) if 0 <= below + j < HALO + LEND]

    clear(fields, vector, HEAD_BLANK, blank_places)
    for i in range(HEAD_BLANK):
        vector[0][i] = with_ones(jnp.zeros((COMPS, TILE), F32))
    for shift, part in enumerate((own, near, far, opposite)):
        g = lax.rem(group[0] + 4 - shift, 4)
        surface[:, pl.ds(pl.multiple_of(g * SUB, SUB), SUB)] = part[...]
        for j in range(HALO):
            residual[LEND + g * HALO + j] = part[:, j * TILE : (j + 1) * TILE]
    products = []
    for g in range(SURF_TILES // HALO):
        rows.wait(g)
        for j in range(HALO):
            products.append(rows.product(vector[0], g, j))
            rows.turn(g, j)
    for i, product in enumerate(products):
        new = residual[LEND + i] / (CENTRE * rows.diagonal(product, i // HALO, i % HALO))
        direction[LEND + i] = new
        total[LEND + i] = new
        vector[0][HALO + LEND + i] = with_ones(new)
    rows.ready.update(range(SURF_TILES // HALO))
    advance(plan, where, LEND, strengths(group[0]), vector, direction, residual, total, range(FAST))


def second_kernel(plan, table, facts_scalars, place, group, film, heat, facts, vectors_in, fields_in, turned,
                  far_hbm, near_hbm, head, edge, vectors, fields, buffer, sems):
    del vectors_in, fields_in
    vector, direction, residual, total = split((vectors, fields), HEAD_ROWS)
    first = (place[0] == 0).astype(F32)

    class LentTable:
        def __getitem__(self, index):
            return facts_scalars[index].astype(jnp.int32)

    def lent_rows(g):
        row = HALO * g + LEND
        ref, row = (far_hbm, row) if row < AHEAD else (near_hbm, row - AHEAD)
        return ref.at[pl.ds(row, HALO)]

    lent = Rows(range(-LEND // HALO, 0), LentTable(), facts.at[pl.ds(SLOTS, LEND)],
                facts.at[pl.ds(SLOTS + LEND, LEND)], LEND, table.shape[1], first, source=lent_rows,
                buffer=buffer, sems=sems)
    fast = Rows((), table, film, heat, 0, 0, turned=turned, turned_groups=range(FAST), ready=range(FAST))

    def where(g):
        return lent if g < 0 else fast

    fetch_all(plan, where)
    advance(plan, where, LEND, strengths(group[0]), vector, direction, residual, total)
    for k in range(0, STEPS, 2):
        for j in range(HALO):
            i = HALO + LEND + j
            a = vector[k][i].astype(F32)[:COMPS]
            b = vector[k + 1][i].astype(F32)[:COMPS] if k + 1 < STEPS else a
            edge[k // 2, j] = jnp.concatenate([a, b], axis=0).astype(BF16)
    for j in range(HEAD):
        head[:, j * TILE : (j + 1) * TILE] = total[LEND + j]


def tail_kernel(plan, table, group, edge, film, heat, head, tiles_hbm, out, vectors, fields, buffer, turned,
                sems):
    vector, direction, residual, total = split((vectors, fields), TAIL)
    row_tiles = out.shape[1] // TILE
    first = row_tiles - TAIL
    groups = range(-TAIL // HALO, 0)
    rows = Rows(groups, table, film, heat, row_tiles, row_tiles, source=rows_from(tiles_hbm, row_tiles),
                buffer=buffer, sems=sems, turned=turned, turned_groups=groups[1:])

    def where(g):
        return rows

    fetch_all(plan, where)

    def blank_places(k):
        below = HALO + TAIL - HALO * (k + 2)
        return [below + j for j in range(2 * HALO)]

    clear(fields, vector, TAIL_BLANK, blank_places)
    for k in range(STEPS):
        for j in range(HALO):
            pair = edge[k // 2, j].astype(F32)
            half = pair[(k % 2) * COMPS : (k % 2 + 1) * COMPS, :]
            vector[k][HALO + TAIL + j] = with_ones(half)
    out[:, : HEAD * TILE] = head[...]
    out[:, HEAD * TILE : first * TILE] = jnp.zeros((COMPS, (first - HEAD) * TILE), F32)
    advance(plan, where, TAIL, strengths(group[0]), vector, direction, residual, total)
    for j in range(TAIL):
        out[:, (first + j) * TILE : (first + j + 1) * TILE] = total[j]


def vmem():
    return pl.BlockSpec(memory_space=pltpu.VMEM)


def smem():
    return pl.BlockSpec(memory_space=pltpu.SMEM)


def hbm():
    return pl.BlockSpec(memory_space=pltpu.HBM)


def in_hbm(*arrays):
    return [pltpu.with_memory_space_constraint(a, pltpu.HBM) for a in arrays]


def work(gigaflops):
    return pl.CostEstimate(flops=gigaflops * 10**9, bytes_accessed=0, transcendentals=0)


def kernel_params(mib):
    return pltpu.CompilerParams(vmem_limit_bytes=mib << 20)


def local(
    boundary_power_density,
    face_scales,
    face_node,
    send_counts,
    tile_values,
    tile_mask,
    tile_columns,
    film_sink,
    capacity,
):
    parts = lax.axis_size("space")
    groups = lax.axis_size("freq")
    place = lax.axis_index("space")
    group = lax.axis_index("freq").astype(jnp.int32).reshape(1)
    nodes_here = film_sink.shape[0]
    row_tiles = nodes_here // TILE
    up = [(i, i + 1) for i in range(parts - 1)]
    down = [(i + 1, i) for i in range(parts - 1)]
    first_plan, second_plan = head_plan()
    assert groups == 4

    tile_values = pltpu.with_memory_space_constraint(tile_values, pltpu.HBM)
    film = film_sink.reshape(row_tiles, TILE)
    heat = capacity.reshape(row_tiles, TILE)
    columns, mask = tile_columns.T, tile_mask.T

    def array(shape, dtype=F32):
        return jax.ShapeDtypeStruct(shape, dtype)

    packed, head_table, tail_table, facts, far = pl.pallas_call(
        pack_kernel,
        out_shape=(
            pltpu.HBM((parts, PACK, TILE), BF16),
            pltpu.HBM((SLOTS, row_tiles), jnp.int32),
            pltpu.HBM((SLOTS, row_tiles), jnp.int32),
            pltpu.HBM((SLOTS + 2 * LEND, TILE), F32),
            pltpu.HBM((AHEAD, SLOTS, TILE, TILE), BF16),
        ),
        in_specs=[smem()] + [vmem()] * 7 + [hbm()],
        out_specs=(vmem(),) * 5,
        scratch_shapes=[pltpu.SemaphoreType.DMA((AHEAD,))],
        compiler_params=kernel_params(8),
        name="pack",
    )(
        send_counts,
        *in_hbm(
            boundary_power_density,
            face_scales.reshape(parts, TILE),
            face_node.reshape(parts, TILE),
            mask,
            columns,
            film,
            heat,
        ),
        tile_values,
    )
    got = lax.all_to_all(packed, "space", 0, 0)

    near = pl.pallas_call(
        lend_kernel,
        out_shape=array((LEND - AHEAD, SLOTS, TILE, TILE), BF16),
        in_specs=[hbm()],
        out_specs=vmem(),
        scratch_shapes=[pltpu.SemaphoreType.DMA((LEND - AHEAD,))],
        compiler_params=kernel_params(8),
        cost_estimate=pl.CostEstimate(flops=0, bytes_accessed=6 << 20, transcendentals=0),
        name="lend",
    )(tile_values)
    far, near = (lax.ppermute(piece, "space", up) for piece in (far, near))
    facts = lax.ppermute(facts, "space", up)

    parts_of = pl.pallas_call(
        scatter_kernel,
        out_shape=(pltpu.HBM((COMPS, SUB), F32),) * groups,
        in_specs=[smem(), vmem(), vmem()],
        out_specs=(vmem(),) * groups,
        scratch_shapes=[pltpu.VMEM((LEVELS, SUB), F32)] * 2,
        compiler_params=kernel_params(8),
        name="scatter",
    )(group, jnp.asarray(fourier_table()), got)
    mixed = [parts_of[0]] + [
        lax.ppermute(parts_of[s], "freq", [(i, (i + s) % groups) for i in range(groups)])
        for s in range(1, groups)
    ]

    held = state_shape(HEAD_ROWS)
    groups_here = HEAD // HALO

    def tile_buffer(count):
        return pltpu.VMEM((count * HALO, SLOTS, TILE, TILE), BF16)

    held_shape = [pltpu.VMEM(*h) for h in held]
    surface, *state, turned = pl.pallas_call(
        lambda *refs: first_kernel(first_plan, *refs),
        out_shape=(
            array((COMPS, SURF_TILES * TILE)),
            *held_shape,
            pltpu.VMEM((TURNED * HALO, SLOTS, TILE, TILE), BF16),
        ),
        in_specs=[smem()] * 2 + [vmem()] * 6 + [hbm(), pl.BlockSpec(memory_space=pl.ANY)],
        out_specs=(vmem(),) * 4,
        scratch_shapes=[
            tile_buffer(groups_here),
            pltpu.SemaphoreType.DMA((groups_here,)),
        ],
        compiler_params=kernel_params(24),
        cost_estimate=work(20),
        name="first",
    )(
        *in_hbm(head_table),
        group,
        *mixed,
        *in_hbm(film, heat),
        tile_values,
        far,
    )

    head, edge, *_ = pl.pallas_call(
        lambda *refs: second_kernel(second_plan, *refs),
        out_shape=(
            array((COMPS, HEAD * TILE)),
            array(((STEPS + 1) // 2, HALO, 2 * COMPS, TILE), BF16),
            *held_shape,
        ),
        in_specs=[smem()] * 4 + [vmem()] * 6 + [pl.BlockSpec(memory_space=pl.ANY)] * 2,
        out_specs=(vmem(),) * 4,
        scratch_shapes=[
            tile_buffer(LEND // HALO),
            pltpu.SemaphoreType.DMA((LEND // HALO,)),
        ],
        input_output_aliases={7: 2, 8: 3},
        compiler_params=kernel_params(16),
        name="second",
    )(
        head_table,
        facts,
        place.astype(jnp.int32).reshape(1),
        group,
        film,
        heat,
        facts,
        *[pltpu.with_memory_space_constraint(x, pltpu.VMEM) for x in (*state, turned)],
        far,
        near,
    )
    edge = lax.ppermute(edge, "space", down)

    temperature = pl.pallas_call(
        lambda *refs: tail_kernel(tail_plan(), *refs),
        out_shape=array((COMPS, nodes_here)),
        in_specs=[smem()] * 2 + [vmem()] * 4 + [hbm()],
        out_specs=vmem(),
        scratch_shapes=[
            *[pltpu.VMEM(*h) for h in state_shape(TAIL)],
            tile_buffer(TAIL // HALO),
            tile_buffer(TAIL // HALO - 1),
            pltpu.SemaphoreType.DMA((TAIL // HALO,)),
        ],
        compiler_params=kernel_params(24),
        name="tail",
    )(tail_table, group, edge, film, heat, head, tile_values)
    return surface, temperature


def solution(mesh):
    placed = (
        P(None, ("freq", "space")),
        P(("freq", "space")),
        P(("freq", "space")),
        P(("freq", "space")),
        P("space", None, None, None),
        P("space", None),
        P("space", None),
        P("space"),
        P("space"),
    )
    return jax.shard_map(
        local,
        mesh=mesh,
        in_specs=placed,
        out_specs=(P("freq", "space"), P("freq", "space")),
        check_vma=False,
    )
```

```python
import math

import jax
import jax.numpy as jnp
import numpy as np
from jax import lax
from jax.experimental import pallas as pl
from jax.experimental.pallas import tpu as pltpu
from jax.sharding import PartitionSpec as P

SUB = 512
TILE = 128
SLOTS = 8
HALO = 4
SWEEPS = 8
COMPS = 8
LEVELS = 32

LOW_EDGE = 0.05
HIGH_EDGE = 2.0
FREQUENCY_SPACING = 0.003

STEPS = SWEEPS - 1
SURF_TILES = 16
HEAD = SURF_TILES + HALO * STEPS
TAIL = HALO * STEPS
LEND = 12
AHEAD = 4
PACK = 48

HEAD_ROWS = LEND + HEAD
HEAD_BLANK = HEAD_ROWS + 2 * HALO
TAIL_BLANK = TAIL + 2 * HALO

F32 = jnp.float32
BF16 = jnp.bfloat16


def fourier_table():
    row = np.arange(LEVELS)
    p = (row // 2).astype(np.float64)[:, None]
    n = np.arange(LEVELS, dtype=np.float64)[None, :]
    angle = 2.0 * math.pi / LEVELS * p * n
    even = np.where(p == 0, 1.0 / LEVELS, 2.0 / LEVELS * np.cos(angle))
    odd = np.where(p == 0, np.cos(math.pi * n) / LEVELS, -2.0 / LEVELS * np.sin(angle))
    return np.where((row % 2 == 1)[:, None], odd, even).astype(np.float32)


CENTRE = 0.5 * (HIGH_EDGE + LOW_EDGE)


def chebyshev_scalars():
    half = 0.5 * (HIGH_EDGE - LOW_EDGE)
    stretch = CENTRE / half
    previous = 1.0 / stretch
    scalars = []
    for _ in range(STEPS):
        current = 1.0 / (2.0 * stretch - previous)
        scalars.append((current * previous, 2.0 * current / half))
        previous = current
    return scalars


def needs(task, low, high):
    k, g = task
    if k == 1:
        return []
    return [(k - 1, h) for h in (g - 1, g, g + 1) if low(k - 1) <= h <= high(k - 1)]


def in_order(tasks):
    steps = sorted({k for k, _ in tasks})
    return [sorted(t for t in tasks if t[0] == k) for k in steps]


def head_plan():
    def low(k):
        return -min(k, STEPS - k)

    def high(k):
        return 3 + k

    def reads(task):
        return needs(task, lambda k: -k, high)

    every = {(k, g) for k in range(1, STEPS + 1) for g in range(low(k), high(k) + 1)}
    free = set()
    for task in sorted(every):
        if task[1] >= 0 and all(n in free for n in reads(task)):
            free.add(task)
    return in_order(free), in_order(every - free)


def tail_plan():
    return [[(k, g) for g in range(-k, 0)] for k in range(1, STEPS + 1)]


def copy_rows(tiles_hbm, first, out, sems):
    copies = []
    for n in range(out.shape[0]):
        copies.append(pltpu.make_async_copy(tiles_hbm.at[first + n], out.at[n], sems.at[n]))
        copies[-1].start()
    return copies


def lend_kernel(tiles_hbm, after, near, sems):
    del after
    for copy in copy_rows(tiles_hbm, tiles_hbm.shape[0] - LEND + AHEAD, near, sems):
        copy.wait()


def pack_kernel(counts, power, scales, nodes, mask, columns, film, heat, tiles_hbm, out, head_table, tail_table,
                facts, far, sems):
    row_tiles = film.shape[0]
    targets = out.shape[0]
    copies = copy_rows(tiles_hbm, row_tiles - LEND, far, sems)
    row = lax.broadcasted_iota(jnp.int32, (16, TILE), 0)
    lane = lax.broadcasted_iota(jnp.int32, (16, TILE), 1)
    for d in range(targets):
        out[d, :LEVELS, :] = power[:, d * TILE : (d + 1) * TILE]
        scale = jnp.broadcast_to(scales[d : d + 1, :].astype(F32), (16, TILE))
        node = jnp.broadcast_to(nodes[d : d + 1, :], (16, TILE))
        weight = jnp.where(lane < counts[d], scale, 0.0)
        high = (node >> 5).astype(F32)
        low = (node & 31).astype(F32)
        aux = jnp.where(row == 0, weight, jnp.where(row == 1, high, low))
        out[d, LEVELS:, :] = aux.astype(BF16)
    live = mask[...] > 0
    head_table[...] = jnp.where(live, columns[...] + LEND, HEAD_BLANK)
    tail_table[...] = jnp.where(live, columns[...] - (row_tiles - TAIL), TAIL_BLANK)
    lent_table = jnp.where(live, columns[...] - (row_tiles - LEND), HEAD_BLANK)
    facts[:SLOTS, :] = lent_table.astype(F32)
    facts[SLOTS : SLOTS + LEND, :] = film[row_tiles - LEND :, :]
    facts[SLOTS + LEND :, :] = heat[row_tiles - LEND :, :]
    for copy in copies:
        copy.wait()


def scatter_kernel(group, table, got, *rest):
    out, (sums, surface) = rest[:-2], rest[-2:]
    sources = got.shape[0]
    span = 8
    place = lax.broadcasted_iota(jnp.int32, (SUB, TILE), 0).astype(F32)

    def spread(s):
        aux = got[s, LEVELS:, :].astype(F32)
        node = aux[1:2, :] * 32.0 + aux[2:3, :]
        weight = jnp.broadcast_to(aux[0:1, :], (SUB, TILE))
        hit = jnp.broadcast_to(node, (SUB, TILE)) == place
        return jnp.where(hit, weight, 0.0).astype(BF16)

    sums[...] = jnp.zeros((LEVELS, SUB), F32)

    def body(i, carry):
        first = i * span
        left = jnp.concatenate([got[first + n, :LEVELS, :] for n in range(span)], axis=1)
        right = jnp.concatenate([spread(first + n) for n in range(span)], axis=1)
        sums[...] += lax.dot_general(
            left, right, (((1,), (1,)), ((), ())), preferred_element_type=F32
        )
        return carry

    lax.fori_loop(0, sources // span, body, 0)
    surface[...] = jnp.dot(
        table[...], sums[...], precision=lax.Precision.HIGHEST, preferred_element_type=F32
    )
    for shift in range(len(out)):
        f = lax.rem(group[0] + shift, len(out))
        out[shift][...] = surface[pl.ds(pl.multiple_of(f * COMPS, COMPS), COMPS), :]


def with_ones(v):
    return jnp.concatenate([v, jnp.ones((COMPS, TILE), F32)], axis=0).astype(BF16)


def rotated(v):
    even = lax.broadcasted_iota(jnp.int32, v.shape, 0) % 2 == 0
    return jnp.where(even, -pltpu.roll(v, COMPS - 1, 0), pltpu.roll(v, 1, 0))


def strengths(group):
    comp = lax.broadcasted_iota(jnp.int32, (COMPS, TILE), 0) + group * COMPS
    return FREQUENCY_SPACING * (comp // 2).astype(F32)


class Rows:
    def __init__(self, groups, table, film, heat, fact_row, table_row, extra=0.0, source=None, buffer=None,
                 sems=None, turned=None, turned_groups=(), ready=()):
        self.table, self.film, self.heat = table, film, heat
        self.fact_row, self.table_row, self.extra = fact_row, table_row, extra
        self.buffer, self.turned, self.ready = buffer, turned, set(ready)
        self.turned_slot = {g: n * HALO for n, g in enumerate(turned_groups)}
        self.slot, self.copies = {}, {}
        if source is not None:
            for n, g in enumerate(groups):
                self.slot[g] = n * HALO
                self.copies[g] = pltpu.make_async_copy(
                    source(g), buffer.at[pl.ds(n * HALO, HALO)], sems.at[n]
                )

    def fetch(self, g):
        if g in self.copies:
            self.copies[g].start()

    def wait(self, g):
        copy = self.copies.pop(g, None)
        if copy is not None:
            copy.wait()

    def turn(self, g, j):
        for t in range(SLOTS):
            self.turned[self.turned_slot[g] + j, t] = self.buffer[self.slot[g] + j, t].T

    def product(self, vector, g, j):
        row = HALO * g + j + self.table_row
        left = jnp.concatenate([vector[self.table[t, row]] for t in range(SLOTS)], axis=1)
        if g in self.ready:
            i = self.turned_slot[g] + j
            right = jnp.concatenate([self.turned[i, t] for t in range(SLOTS)], axis=0)
        else:
            i = self.slot[g] + j
            right = jnp.concatenate([self.buffer[i, t] for t in range(SLOTS)], axis=1)
        side = 0 if g in self.ready else 1
        return lax.dot_general(
            left, right, (((1,), (side,)), ((), ())), preferred_element_type=F32
        )

    def diagonal(self, product, g, j):
        row = HALO * g + j + self.fact_row
        return product[COMPS:, :] + (self.film[row : row + 1, :] + self.extra)

    def shift(self, strength, g, j):
        row = HALO * g + j + self.fact_row
        return strength * self.heat[row : row + 1, :]


def rows_from(ref, row):
    return lambda g: ref.at[pl.ds(HALO * g + row, HALO)]


def fetch_all(plan, where):
    seen = set()
    for tasks in plan:
        for _, g in tasks:
            if g not in seen:
                seen.add(g)
                where(g).fetch(g)


def advance(plan, where, shift, strength, vectors, direction, residual, total, keep_turned=(), rate=2):
    scalars = chebyshev_scalars()
    for n_step, tasks in enumerate(plan):
        k = tasks[0][0]
        keep, gain = scalars[k - 1]
        later = [g for step in plan[n_step + 1 :] for _, g in step] + list(keep_turned)
        fetched = {g for step in plan[: n_step + 1] for _, g in step}
        wanted = [
            g for g in fetched if g in later and g in where(g).turned_slot and g not in where(g).ready
        ]
        wanted = sorted(wanted, key=lambda g: -later.count(g))[:rate]
        turns = [(g, j) for g in wanted for j in range(HALO)]
        products = []
        for n, (_, g) in enumerate(tasks):
            where(g).wait(g)
            products += [where(g).product(vectors[k - 1], g, j) for j in range(HALO)]
            share = -(-len(turns) // len(tasks))
            for h, j in [t for t in turns[n * share : (n + 1) * share]]:
                where(h).wait(h)
                where(h).turn(h, j)
        for g in wanted:
            where(g).ready.add(g)
        for n, (_, g) in enumerate(tasks):
            for j in range(HALO):
                product, state = products[n * HALO + j], HALO * g + j + shift
                diag = where(g).diagonal(product, g, j)
                v = direction[state]
                mv = diag * v - product[:COMPS, :] + where(g).shift(strength, g, j) * rotated(v)
                r = residual[state] - mv
                new = keep * v + gain * r / diag
                total[state] = total[state] + new
                if k < STEPS:
                    residual[state] = r
                    direction[state] = new
                    vectors[k][HALO + state] = with_ones(new)
    for g in keep_turned:
        if g not in where(g).ready:
            for j in range(HALO):
                where(g).turn(g, j)


def split(refs, rows):
    vectors, fields = refs
    places = rows + 2 * HALO + 1
    return (
        [vectors.at[pl.ds(k * places, places)] for k in range(STEPS)],
        *[fields.at[pl.ds(n * rows, rows)] for n in range(3)],
    )


def state_shape(rows):
    return [
        ((STEPS * (rows + 2 * HALO + 1), 2 * COMPS, TILE), BF16),
        ((3 * rows, COMPS, TILE), F32),
    ]


def clear(fields, vectors, blank_place, blank_places):
    zero = jnp.zeros((COMPS, TILE), F32)

    def body(i, carry):
        fields[i] = zero
        return carry

    lax.fori_loop(0, fields.shape[0], body, 0)
    for k, vector in enumerate(vectors):
        vector[blank_place] = jnp.zeros((2 * COMPS, TILE), BF16)
        for place in blank_places(k):
            vector[place] = with_ones(zero)


FAST = 6
TURNED = 9


def first_kernel(plan, table, group, own, near, far, opposite, film, heat, tiles_hbm, after, surface, vectors, fields,
                 turned, buffer, sems):
    del after
    vector, direction, residual, total = split((vectors, fields), HEAD_ROWS)
    groups = range(HEAD // HALO)
    rows = Rows(groups, table, film, heat, 0, 0, source=rows_from(tiles_hbm, 0), buffer=buffer, sems=sems,
                turned=turned, turned_groups=groups[:TURNED])

    def where(g):
        return rows

    fetch_all(plan, where)

    def blank_places(k):
        above = HALO + LEND + SURF_TILES + HALO * k
        below = HALO + LEND - HALO * (k + 2)
        places = [0] + [above + j for j in range(2 * HALO)]
        return places + [below + j for j in range(2 * HALO) if 0 <= below + j < HALO + LEND]

    clear(fields, vector, HEAD_BLANK, blank_places)
    for i in range(HEAD_BLANK):
        vector[0][i] = with_ones(jnp.zeros((COMPS, TILE), F32))
    for shift, part in enumerate((own, near, far, opposite)):
        g = lax.rem(group[0] + 4 - shift, 4)
        surface[:, pl.ds(pl.multiple_of(g * SUB, SUB), SUB)] = part[...]
        for j in range(HALO):
            residual[LEND + g * HALO + j] = part[:, j * TILE : (j + 1) * TILE]
    products = []
    for g in range(SURF_TILES // HALO):
        rows.wait(g)
        for j in range(HALO):
            products.append(rows.product(vector[0], g, j))
            rows.turn(g, j)
    for i, product in enumerate(products):
        new = residual[LEND + i] / (CENTRE * rows.diagonal(product, i // HALO, i % HALO))
        direction[LEND + i] = new
        total[LEND + i] = new
        vector[0][HALO + LEND + i] = with_ones(new)
    rows.ready.update(range(SURF_TILES // HALO))
    advance(plan, where, LEND, strengths(group[0]), vector, direction, residual, total, range(FAST))


def second_kernel(plan, table, facts_scalars, place, group, film, heat, facts, vectors_in, fields_in, turned,
                  far_hbm, near_hbm, head, edge, vectors, fields, buffer, sems):
    del vectors_in, fields_in
    vector, direction, residual, total = split((vectors, fields), HEAD_ROWS)
    first = (place[0] == 0).astype(F32)

    class LentTable:
        def __getitem__(self, index):
            return facts_scalars[index].astype(jnp.int32)

    def lent_rows(g):
        row = HALO * g + LEND
        ref, row = (far_hbm, row) if row < AHEAD else (near_hbm, row - AHEAD)
        return ref.at[pl.ds(row, HALO)]

    lent = Rows(range(-LEND // HALO, 0), LentTable(), facts.at[pl.ds(SLOTS, LEND)],
                facts.at[pl.ds(SLOTS + LEND, LEND)], LEND, table.shape[1], first, source=lent_rows,
                buffer=buffer, sems=sems)
    fast = Rows((), table, film, heat, 0, 0, turned=turned, turned_groups=range(FAST), ready=range(FAST))

    def where(g):
        return lent if g < 0 else fast

    fetch_all(plan, where)
    advance(plan, where, LEND, strengths(group[0]), vector, direction, residual, total)
    for k in range(0, STEPS, 2):
        for j in range(HALO):
            i = HALO + LEND + j
            a = vector[k][i].astype(F32)[:COMPS]
            b = vector[k + 1][i].astype(F32)[:COMPS] if k + 1 < STEPS else a
            edge[k // 2, j] = jnp.concatenate([a, b], axis=0).astype(BF16)
    for j in range(HEAD):
        head[:, j * TILE : (j + 1) * TILE] = total[LEND + j]


def tail_kernel(plan, table, group, edge, film, heat, head, tiles_hbm, out, vectors, fields, buffer, turned,
                sems):
    vector, direction, residual, total = split((vectors, fields), TAIL)
    row_tiles = out.shape[1] // TILE
    first = row_tiles - TAIL
    groups = range(-TAIL // HALO, 0)
    rows = Rows(groups, table, film, heat, row_tiles, row_tiles, source=rows_from(tiles_hbm, row_tiles),
                buffer=buffer, sems=sems, turned=turned, turned_groups=groups[1:])

    def where(g):
        return rows

    fetch_all(plan, where)

    def blank_places(k):
        below = HALO + TAIL - HALO * (k + 2)
        return [below + j for j in range(2 * HALO)]

    clear(fields, vector, TAIL_BLANK, blank_places)
    for k in range(STEPS):
        for j in range(HALO):
            pair = edge[k // 2, j].astype(F32)
            half = pair[(k % 2) * COMPS : (k % 2 + 1) * COMPS, :]
            vector[k][HALO + TAIL + j] = with_ones(half)
    out[:, : HEAD * TILE] = head[...]
    out[:, HEAD * TILE : first * TILE] = jnp.zeros((COMPS, (first - HEAD) * TILE), F32)
    advance(plan, where, TAIL, strengths(group[0]), vector, direction, residual, total)
    for j in range(TAIL):
        out[:, (first + j) * TILE : (first + j + 1) * TILE] = total[j]


def vmem():
    return pl.BlockSpec(memory_space=pltpu.VMEM)


def smem():
    return pl.BlockSpec(memory_space=pltpu.SMEM)


def hbm():
    return pl.BlockSpec(memory_space=pltpu.HBM)


def in_hbm(*arrays):
    return [pltpu.with_memory_space_constraint(a, pltpu.HBM) for a in arrays]


def work(gigaflops):
    return pl.CostEstimate(flops=gigaflops * 10**9, bytes_accessed=0, transcendentals=0)


def kernel_params(mib):
    return pltpu.CompilerParams(vmem_limit_bytes=mib << 20)


def local(
    boundary_power_density,
    face_scales,
    face_node,
    send_counts,
    tile_values,
    tile_mask,
    tile_columns,
    film_sink,
    capacity,
):
    parts = lax.axis_size("space")
    groups = lax.axis_size("freq")
    place = lax.axis_index("space")
    group = lax.axis_index("freq").astype(jnp.int32).reshape(1)
    nodes_here = film_sink.shape[0]
    row_tiles = nodes_here // TILE
    up = [(i, i + 1) for i in range(parts - 1)]
    down = [(i + 1, i) for i in range(parts - 1)]
    first_plan, second_plan = head_plan()
    assert groups == 4

    tile_values = pltpu.with_memory_space_constraint(tile_values, pltpu.HBM)
    film = film_sink.reshape(row_tiles, TILE)
    heat = capacity.reshape(row_tiles, TILE)
    columns, mask = tile_columns.T, tile_mask.T

    def array(shape, dtype=F32):
        return jax.ShapeDtypeStruct(shape, dtype)

    packed, head_table, tail_table, facts, far = pl.pallas_call(
        pack_kernel,
        out_shape=(
            pltpu.HBM((parts, PACK, TILE), BF16),
            pltpu.HBM((SLOTS, row_tiles), jnp.int32),
            pltpu.HBM((SLOTS, row_tiles), jnp.int32),
            pltpu.HBM((SLOTS + 2 * LEND, TILE), F32),
            pltpu.HBM((AHEAD, SLOTS, TILE, TILE), BF16),
        ),
        in_specs=[smem()] + [vmem()] * 7 + [hbm()],
        out_specs=(vmem(),) * 5,
        scratch_shapes=[pltpu.SemaphoreType.DMA((AHEAD,))],
        compiler_params=kernel_params(8),
        name="pack",
    )(
        send_counts,
        *in_hbm(
            boundary_power_density,
            face_scales.reshape(parts, TILE),
            face_node.reshape(parts, TILE),
            mask,
            columns,
            film,
            heat,
        ),
        tile_values,
    )
    got = lax.all_to_all(packed, "space", 0, 0)

    facts = lax.ppermute(facts, "space", up)
    near = pl.pallas_call(
        lend_kernel,
        out_shape=array((LEND - AHEAD, SLOTS, TILE, TILE), BF16),
        in_specs=[hbm(), pl.BlockSpec(memory_space=pl.ANY)],
        out_specs=vmem(),
        scratch_shapes=[pltpu.SemaphoreType.DMA((LEND - AHEAD,))],
        compiler_params=kernel_params(8),
        cost_estimate=pl.CostEstimate(flops=0, bytes_accessed=6 << 20, transcendentals=0),
        name="lend",
    )(tile_values, facts)
    far, near = (lax.ppermute(piece, "space", up) for piece in (far, near))

    parts_of = pl.pallas_call(
        scatter_kernel,
        out_shape=(pltpu.HBM((COMPS, SUB), F32),) * groups,
        in_specs=[smem(), vmem(), vmem()],
        out_specs=(vmem(),) * groups,
        scratch_shapes=[pltpu.VMEM((LEVELS, SUB), F32)] * 2,
        compiler_params=kernel_params(8),
        name="scatter",
    )(group, jnp.asarray(fourier_table()), got)
    mixed = [parts_of[0]] + [
        lax.ppermute(parts_of[s], "freq", [(i, (i + s) % groups) for i in range(groups)])
        for s in range(1, groups)
    ]

    held = state_shape(HEAD_ROWS)
    groups_here = HEAD // HALO

    def tile_buffer(count):
        return pltpu.VMEM((count * HALO, SLOTS, TILE, TILE), BF16)

    held_shape = [pltpu.VMEM(*h) for h in held]
    surface, *state, turned = pl.pallas_call(
        lambda *refs: first_kernel(first_plan, *refs),
        out_shape=(
            array((COMPS, SURF_TILES * TILE)),
            *held_shape,
            pltpu.VMEM((TURNED * HALO, SLOTS, TILE, TILE), BF16),
        ),
        in_specs=[smem()] * 2 + [vmem()] * 6 + [hbm(), pl.BlockSpec(memory_space=pl.ANY)],
        out_specs=(vmem(),) * 4,
        scratch_shapes=[
            tile_buffer(groups_here),
            pltpu.SemaphoreType.DMA((groups_here,)),
        ],
        compiler_params=kernel_params(24),
        cost_estimate=work(20),
        name="first",
    )(
        *in_hbm(head_table),
        group,
        *mixed,
        *in_hbm(film, heat),
        tile_values,
        far,
    )

    head, edge, *_ = pl.pallas_call(
        lambda *refs: second_kernel(second_plan, *refs),
        out_shape=(
            array((COMPS, HEAD * TILE)),
            array(((STEPS + 1) // 2, HALO, 2 * COMPS, TILE), BF16),
            *held_shape,
        ),
        in_specs=[smem()] * 4 + [vmem()] * 6 + [pl.BlockSpec(memory_space=pl.ANY)] * 2,
        out_specs=(vmem(),) * 4,
        scratch_shapes=[
            tile_buffer(LEND // HALO),
            pltpu.SemaphoreType.DMA((LEND // HALO,)),
        ],
        input_output_aliases={7: 2, 8: 3},
        compiler_params=kernel_params(16),
        name="second",
    )(
        head_table,
        facts,
        place.astype(jnp.int32).reshape(1),
        group,
        film,
        heat,
        facts,
        *[pltpu.with_memory_space_constraint(x, pltpu.VMEM) for x in (*state, turned)],
        far,
        near,
    )
    edge = lax.ppermute(edge, "space", down)

    temperature = pl.pallas_call(
        lambda *refs: tail_kernel(tail_plan(), *refs),
        out_shape=array((COMPS, nodes_here)),
        in_specs=[smem()] * 2 + [vmem()] * 4 + [hbm()],
        out_specs=vmem(),
        scratch_shapes=[
            *[pltpu.VMEM(*h) for h in state_shape(TAIL)],
            tile_buffer(TAIL // HALO),
            tile_buffer(TAIL // HALO - 1),
            pltpu.SemaphoreType.DMA((TAIL // HALO,)),
        ],
        compiler_params=kernel_params(24),
        name="tail",
    )(tail_table, group, edge, film, heat, head, tile_values)
    return surface, temperature


def solution(mesh):
    placed = (
        P(None, ("freq", "space")),
        P(("freq", "space")),
        P(("freq", "space")),
        P(("freq", "space")),
        P("space", None, None, None),
        P("space", None),
        P("space", None),
        P("space"),
        P("space"),
    )
    return jax.shard_map(
        local,
        mesh=mesh,
        in_specs=placed,
        out_specs=(P("freq", "space"), P("freq", "space")),
        check_vma=False,
    )
```
